512 devices in a mesh: row: 16 (over x, y), col: 32 (over z, core).
Axes of the slice: x: 4, y: 4, z: 16, core: 2. Of those that a mesh axis runs over, the one named last changes fastest.
Arguments:
- amplitudes: float32 [2048, 12288], P(('col', 'row')), may hold values from -6 to 6
- integrals: float32 [12288, 16384], P('row', 'col'), may hold values from -0.15625 to 0.15625
- ij_irrep: int32 [2048], replicated, may hold values from 0 to 7, as said below
- cd_irrep: int32 [12288], P('row'), may hold values from 0 to 7, as said below
- ab_irrep: int32 [16384], P('col'), may hold values from 0 to 7, as said below
Outputs:
- ladder: float32 [2048, 16384], P('row', 'col')
The draws below stay inside these ranges and needn't reach their ends.
Inputs may be any that keep to these rules, and one draw needn't show every extreme that they name: `ij_irrep`: irrep labels of D2h. `cd_irrep`: irrep labels of D2h. `ab_irrep`: irrep labels of D2h.
All inputs are finite; a program needn't handle non-finite values.
Results may differ from the reference program's by a relative error of at most 0.00009.
Values sent between devices are 32-bit elements; how exact they have to be, the bound alone decides.
No kernel may reach another device: no remote copies, remote signals or barrier semaphores. Data moves between devices by JAX's collectives and lax.ppermute only.
A program may use at most 64 MiB of HBM per device.

```python
import jax
import jax.numpy as jnp
from jax import lax

P_DEV = 4
F_ROW = 768
AB_DEV = 512
PAIRS = 2048
CD = 12288
AB = 16384


def group_labels(key, total, run_size):
    key_major, key_share, key_pick, key_roll, key_back = jax.random.split(key, 5)
    groups = total // run_size
    dominant = jax.random.randint(key_major, (groups,), 0, 8)
    shares = jax.random.randint(key_share, (groups,), 10, 101)
    chosen = jax.random.randint(key_pick, (), 0, groups)
    shares = jnp.where(jnp.arange(groups) == chosen, 100, shares)
    rolls = jax.random.randint(key_roll, (groups, run_size), 0, 100)
    background = jax.random.randint(key_back, (groups, run_size), 0, 8)
    labels = jnp.where(rolls < shares[:, None], dominant[:, None], background)
    return labels.reshape(total).astype(jnp.int32)


def draw_ij_irrep(key, part):
    key = jax.random.fold_in(key, 1)
    return group_labels(key, PAIRS, P_DEV * 8)


def draw_cd_irrep(key, part):
    key = jax.random.fold_in(key, 2)
    return group_labels(key, CD, F_ROW)


def draw_ab_irrep(key, part):
    key = jax.random.fold_in(key, 3)
    return group_labels(key, AB, AB_DEV)


def block_scale(own_key, shape, shards, smallest, high):
    def one(dim, blocks):
        steps = jax.random.uniform(jax.random.fold_in(jax.random.fold_in(own_key, 6), dim), (blocks,), jnp.float32, smallest / len(shards), high / len(shards))
        return jnp.repeat(jnp.exp(steps), shape[dim] // blocks).reshape((-1,) + (1,) * (len(shape) - dim - 1))

    gain = one(*shards[0])
    for cut in shards[1:]:
        gain = gain * one(*cut)
    return gain


def noise(stream_key, extent, width, most, cuts=(), kind=jnp.bfloat16):
    factor_of = block_scale(stream_key, extent, cuts, -0.22, 0.18) if cuts else 1.0
    entries = jax.random.normal(stream_key, extent, jnp.float32) * width * factor_of
    return jnp.minimum(jnp.maximum(entries, -most), most).astype(kind)


def setup_inputs(seed: int = 0) -> dict:
    seeds = jax.random.split(jax.random.key(seed), 6)
    return {
        "amplitudes": noise(seeds[0], (PAIRS, CD), 1.0, 6.0, ((0, 512),), jnp.float32),
        "integrals": noise(seeds[1], (CD, AB), (CD // 8) ** -0.5, 0.15625, ((0, 16), (1, 32)), jnp.float32),
        "ij_irrep": draw_ij_irrep(jax.random.fold_in(seeds[5], 71), 0),
        "cd_irrep": draw_cd_irrep(jax.random.fold_in(seeds[5], 71), 0),
        "ab_irrep": draw_ab_irrep(jax.random.fold_in(seeds[5], 71), 0),
    }


def reference(amplitudes, integrals, ij_irrep, cd_irrep, ab_irrep):
    allowed_t = jnp.where(ij_irrep[:, None] == cd_irrep[None, :], amplitudes, jnp.float32(0.0))
    allowed_v = jnp.where(cd_irrep[:, None] == ab_irrep[None, :], integrals, jnp.float32(0.0))
    summed = jnp.dot(allowed_t, allowed_v, precision=lax.Precision.HIGHEST, preferred_element_type=jnp.float32)
    return 0.5 * summed
```

```python
import functools

import jax
import jax.numpy as jnp
from jax import lax
from jax.experimental import pallas as pl
from jax.experimental.pallas import tpu as pltpu
from jax.sharding import Mesh
from jax.sharding import PartitionSpec as P

BLOCK = 128
BLOCKS = 16
LABELS = 8
OWN = 16
HALF = BLOCKS * OWN
SLOTS = 2 * HALF
CD_CORE = 384
CD_DEV = 24
F32, BF16, I32 = jnp.float32, jnp.bfloat16, jnp.int32


def call(kernel, out_shape, in_specs=None, cost=(1_000_000, 1_000_000), **kwargs):
    return pl.pallas_call(
        kernel,
        out_shape=out_shape,
        compiler_params=pltpu.CompilerParams(vmem_limit_bytes=48 * 1024 * 1024),
        cost_estimate=pl.CostEstimate(flops=cost[0], bytes_accessed=cost[1], transcendentals=0),
        **({} if in_specs is None else {"in_specs": in_specs}),
        **kwargs,
    )


def split3(x):
    hi = x.astype(BF16)
    rest = x - hi.astype(F32)
    mid = rest.astype(BF16)
    return hi, mid, (rest - mid.astype(F32)).astype(BF16)


def down(row):
    return jnp.transpose(jnp.broadcast_to(row, (BLOCK, BLOCK)))


def arrival(rows):
    n = lax.broadcasted_iota(I32, (BLOCK, BLOCK), 0)
    p = lax.broadcasted_iota(I32, (BLOCK, BLOCK), 1)
    move = n == ((p >> 2) & 1) * 64 + (p >> 3) * 4 + (p & 3)
    return jnp.dot(rows, move.astype(F32), precision=lax.Precision.HIGHEST, preferred_element_type=F32)


def turn_kernel(place_ref, x_ref, ij_ref, cd_ref, out_ref):
    core, z = place_ref[0], place_ref[1]
    labels = jnp.broadcast_to(ij_ref[pl.ds(z, 1), :], (8, BLOCK)).astype(F32)
    labels = arrival(labels)[0:1, :].astype(I32)
    for j in range(CD_CORE // BLOCK):
        cols = slice(j * BLOCK, (j + 1) * BLOCK)
        cd = down(cd_ref[pl.ds(core * (CD_CORE // BLOCK) + j, 1), :])
        out_ref[cols, :] = jnp.where(cd == labels, jnp.transpose(x_ref[:, cols]), 0.0)


def pack_kernel(round_ref, x_ref, ij_ref, packed_ref, slot_ref):
    ij = ij_ref[...]
    label = lax.broadcasted_iota(I32, (BLOCKS, LABELS, BLOCK), 1)
    same = (jnp.broadcast_to(ij[:, None, :], label.shape) == label).astype(F32)
    upto = lax.broadcasted_iota(I32, (BLOCK, BLOCK), 0) <= lax.broadcasted_iota(I32, (BLOCK, BLOCK), 1)
    count = jnp.dot(
        same.reshape(BLOCKS * LABELS, BLOCK).astype(BF16), upto.astype(BF16), preferred_element_type=F32
    ).reshape(BLOCKS, LABELS, BLOCK)
    excess = jnp.maximum(count[:, :, BLOCK - 1 :] - OWN, 0.0)
    before = jnp.zeros((1, LABELS, 1), F32)
    rows = []
    for b in range(BLOCKS):
        rank = count[b : b + 1] - 1.0
        slot = jnp.where(rank < OWN, rank + b * OWN, rank - OWN + before + HALF)
        rows.append(jnp.sum(slot * same[b : b + 1], axis=1))
        before = before + excess[b : b + 1]
    slots = jnp.concatenate(rows, axis=0)
    slot_ref[...] = slots.astype(I32)
    here = arrival(slots).astype(I32) - round_ref[0] * SLOTS
    want = lax.broadcasted_iota(I32, (SLOTS, 2 * BLOCK), 0)
    total = jnp.zeros((3 * CD_DEV, SLOTS), F32)
    for b in range(0, BLOCKS, 2):
        pair = jnp.concatenate([here[b : b + 1], here[b + 1 : b + 2]], axis=1)
        chosen = jnp.where(want == pair, 1.0, 0.0).astype(BF16)
        x = jnp.concatenate([x_ref[b], x_ref[b + 1]], axis=1)
        parts = jnp.concatenate([p.astype(F32) for p in split3(x)], axis=0).astype(BF16)
        total += lax.dot_general(parts, chosen, (((1,), (1,)), ((), ())), preferred_element_type=F32)
    packed_ref[...] = total[:CD_DEV] + total[CD_DEV : 2 * CD_DEV] + total[2 * CD_DEV :]


def panel_kernel(v_ref, cd_ref, ab_ref, hi_ref, lo_ref):
    for j in range(v_ref.shape[0] // BLOCK):
        cd = down(cd_ref[j : j + 1, :])
        for k in range(v_ref.shape[1] // BLOCK):
            at = (slice(j * BLOCK, (j + 1) * BLOCK), slice(k * BLOCK, (k + 1) * BLOCK))
            v = jnp.where(cd == ab_ref[:, at[1]], v_ref[at], 0.0)
            hi = v.astype(BF16)
            hi_ref[at] = hi
            lo_ref[at] = (v - hi.astype(F32)).astype(BF16)


def product_kernel(place_ref, mine_ref, other_ref, hi_ref, lo_ref, own_ref, shared_ref):
    core = place_ref[0]
    total = None
    for part, half in ((mine_ref, core), (other_ref, 1 - core)):
        rows = pl.ds(pl.multiple_of(half * CD_CORE, CD_CORE), CD_CORE)
        t = part[...]
        t_hi = t.astype(BF16)
        t_lo = (t - t_hi.astype(F32)).astype(BF16)
        for a, b in ((t_hi, hi_ref), (t_hi, lo_ref), (t_lo, hi_ref)):
            term = lax.dot_general(a, b[rows, :], (((0,), (0,)), ((), ())), preferred_element_type=F32)
            total = term if total is None else total + term
    own_ref[...] = total[:HALF]
    shared_ref[...] = total[HALF:]


def spread(a, slots, labels, ab_ref, out_ref):
    chosen = jnp.where(lax.broadcasted_iota(I32, (a.shape[0], BLOCK), 0) == slots, 1.0, 0.0).astype(BF16)
    total = None
    for part in split3(a):
        term = lax.dot_general(chosen, part, (((0,), (0,)), ((), ())), preferred_element_type=F32)
        total = term if total is None else total + term
    ij = down(labels)
    for k in range(out_ref.shape[1] // BLOCK):
        cols = slice(k * BLOCK, (k + 1) * BLOCK)
        out_ref[:, cols] = jnp.where(ij == ab_ref[:, cols], 0.5 * total[:, cols], 0.0)


def first_kernel(place_ref, own_ref, shared_ref, slot_ref, ij_ref, ab_ref, out_ref):
    row = place_ref[2]
    own = own_ref[0]
    for b in range(1, BLOCKS):
        own = own + own_ref[b]
    slots = slot_ref[pl.ds(row, 1), :]
    slots = jnp.where(slots < HALF, slots - row * OWN, slots - HALF + OWN)
    spread(jnp.concatenate([own, shared_ref[...]], axis=0), slots, ij_ref[pl.ds(row, 1), :], ab_ref, out_ref)


def later_kernel(place_ref, round_ref, a_ref, slot_ref, ij_ref, ab_ref, out_ref):
    row = place_ref[2]
    slots = slot_ref[pl.ds(row, 1), :] - round_ref[0] * SLOTS
    spread(a_ref[...], slots, ij_ref[pl.ds(row, 1), :], ab_ref, out_ref)


def body(amplitudes, integrals, ij_irrep, cd_irrep, ab_irrep):
    smem = pl.BlockSpec(memory_space=pltpu.SMEM)
    vmem = pl.BlockSpec(memory_space=pltpu.VMEM)
    shape = jax.ShapeDtypeStruct
    place = jnp.stack([lax.axis_index("core"), lax.axis_index("z"), lax.axis_index("row")]).astype(I32)
    ij = ij_irrep.reshape(BLOCKS, BLOCK)
    cd = cd_irrep.reshape(-1, BLOCK)
    ab = ab_irrep.reshape(1, -1)
    cds, abs_ = integrals.shape

    arrived = lax.all_to_all(amplitudes, ("row", "core"), split_axis=1, concat_axis=0, tiled=True)
    turned = call(turn_kernel, shape((CD_CORE, BLOCK), F32), [smem, vmem, vmem, vmem])(place, arrived, ij, cd)
    mine = lax.all_to_all(turned, "z", split_axis=0, concat_axis=0, tiled=True).reshape(BLOCKS, CD_DEV, BLOCK)

    v_hi, v_lo = call(panel_kernel, [shape((cds, abs_), BF16)] * 2, [vmem] * 3, (2_000_000, 3_200_000))(integrals, cd, ab)

    def products(number):
        packed, slots = call(
            pack_kernel, [shape((CD_DEV, SLOTS), F32), shape((BLOCKS, BLOCK), I32)], [smem, vmem, vmem]
        )(number, mine, ij)
        gathered = lax.all_gather(packed, "z", axis=0, tiled=True)
        other = lax.ppermute(gathered, "core", [(0, 1), (1, 0)])
        own, shared = call(
            product_kernel, [shape((HALF, abs_), F32)] * 2, [smem] + [vmem] * 4, (1_200_000_000, 5_000_000)
        )(place, gathered, other, v_hi, v_lo)
        return own, shared, slots

    own, shared, slots = products(jnp.zeros((1,), I32))
    shared = lax.all_to_all(shared, "row", split_axis=0, concat_axis=0, tiled=True)
    shared = jnp.sum(shared.reshape(BLOCKS, OWN, abs_), axis=0)
    shared = lax.all_gather(shared, "row", axis=0, tiled=True)
    own = lax.all_to_all(own, "row", split_axis=0, concat_axis=0, tiled=True)
    out = call(first_kernel, shape((BLOCK, abs_), F32), [smem] + [vmem] * 5)(
        place, own.reshape(BLOCKS, OWN, abs_), shared, slots, ij, ab
    )
    rounds = (jnp.max(slots) >> 9) + 1

    def again(state):
        number, out = state
        own, shared, slots = products(number[None])
        whole = lax.psum(jnp.concatenate([own, shared], axis=0), "row")
        more = call(later_kernel, shape((BLOCK, abs_), F32), [smem] * 2 + [vmem] * 4)(
            place, number[None], whole, slots, ij, ab
        )
        return number + 1, out + more

    return lax.while_loop(lambda state: state[0] < rounds, again, (jnp.int32(1), out))[1]


def solution(mesh):
    finer = Mesh(mesh.devices.reshape(16, 16, 2), ("row", "z", "core"))
    in_specs = (P(("z", "core", "row"), None), P("row", ("z", "core")), P(), P("row"), P(("z", "core")))
    out_specs = P("row", ("z", "core"))
    return jax.shard_map(body, mesh=finer, in_specs=in_specs, out_specs=out_specs, check_vma=False)
```

```python
import jax
import jax.numpy as jnp
from jax import lax
from jax.experimental import pallas as pl
from jax.experimental.pallas import tpu as pltpu
from jax.sharding import Mesh
from jax.sharding import PartitionSpec as P

BLOCK = 128
BLOCKS = 16
LABELS = 8
OWN = 16
HALF = BLOCKS * OWN
SLOTS = 2 * HALF
CD_CORE = 384
STEP = 4
F32, BF16, I32 = jnp.float32, jnp.bfloat16, jnp.int32


def call(kernel, out_shape, in_specs=None, cost=(1_000_000, 1_000_000), **kwargs):
    return pl.pallas_call(
        kernel,
        out_shape=out_shape,
        compiler_params=pltpu.CompilerParams(vmem_limit_bytes=48 * 1024 * 1024),
        cost_estimate=pl.CostEstimate(flops=cost[0], bytes_accessed=cost[1], transcendentals=0),
        **({} if in_specs is None else {"in_specs": in_specs}),
        **kwargs,
    )


def split3(x):
    hi = x.astype(BF16)
    rest = x - hi.astype(F32)
    mid = rest.astype(BF16)
    return hi, mid, (rest - mid.astype(F32)).astype(BF16)


def down(row):
    return jnp.transpose(jnp.broadcast_to(row, (BLOCK, BLOCK)))


def arrival(rows):
    n = lax.broadcasted_iota(I32, (BLOCK, BLOCK), 0)
    p = lax.broadcasted_iota(I32, (BLOCK, BLOCK), 1)
    move = n == ((p >> 2) & 1) * 64 + (p >> 3) * 4 + (p & 3)
    return jnp.dot(rows, move.astype(F32), precision=lax.Precision.HIGHEST, preferred_element_type=F32)


def turn_kernel(place_ref, x_ref, ij_ref, cd_ref, out_ref):
    core, z = place_ref[0], place_ref[1]
    labels = jnp.broadcast_to(ij_ref[pl.ds(z, 1), :], (8, BLOCK)).astype(F32)
    labels = arrival(labels)[0:1, :].astype(I32)
    for j in range(CD_CORE // BLOCK):
        cols = slice(j * BLOCK, (j + 1) * BLOCK)
        cd = down(cd_ref[pl.ds(core * (CD_CORE // BLOCK) + j, 1), :])
        out_ref[cols, :] = jnp.where(cd == labels, jnp.transpose(x_ref[:, cols]), 0.0)


def table_kernel(round_ref, ij_ref, slot_ref, chosen_ref):
    ij = ij_ref[...]
    label = lax.broadcasted_iota(I32, (BLOCKS, LABELS, BLOCK), 1)
    same = (jnp.broadcast_to(ij[:, None, :], label.shape) == label).astype(F32)
    upto = lax.broadcasted_iota(I32, (BLOCK, BLOCK), 0) <= lax.broadcasted_iota(I32, (BLOCK, BLOCK), 1)
    count = jnp.dot(
        same.reshape(BLOCKS * LABELS, BLOCK).astype(BF16), upto.astype(BF16), preferred_element_type=F32
    ).reshape(BLOCKS, LABELS, BLOCK)
    excess = jnp.maximum(count[:, :, BLOCK - 1 :] - OWN, 0.0)
    before = jnp.zeros((1, LABELS, 1), F32)
    own_rows, over_rows = [], []
    for b in range(BLOCKS):
        rank = count[b : b + 1] - 1.0
        over = jnp.where(rank < OWN, -1.0, rank - OWN + before)
        own_rows.append(jnp.sum(rank * same[b : b + 1], axis=1) + b * 2 * OWN)
        over_rows.append(jnp.sum(over * same[b : b + 1], axis=1))
        before = before + excess[b : b + 1]
    own = jnp.concatenate(own_rows, axis=0).astype(I32)
    over = jnp.concatenate(over_rows, axis=0).astype(I32)
    shared = (over >> 4) * (2 * OWN) + OWN + (over & (OWN - 1))
    slots = jnp.where(over < 0, own, jnp.where(over < HALF, shared, over + HALF))
    slot_ref[...] = slots
    here = arrival(slots.astype(F32)).astype(I32) - round_ref[0] * SLOTS
    want = lax.broadcasted_iota(I32, (SLOTS, BLOCK), 0)
    for b in range(BLOCKS):
        chosen_ref[:, b * BLOCK : (b + 1) * BLOCK] = jnp.where(want == here[b : b + 1], 1.0, 0.0).astype(BF16)


def pack_kernel(x_ref, chosen_ref, packed_ref):
    @pl.when(pl.program_id(0) == 0)
    def _():
        packed_ref[...] = jnp.zeros_like(packed_ref)

    x = jnp.concatenate([x_ref[b] for b in range(STEP)], axis=1)
    hi = x.astype(BF16)
    lo = (x - hi.astype(F32)).astype(BF16)
    dims = (((1,), (1,)), ((), ()))
    packed_ref[...] += lax.dot_general(hi, chosen_ref[...], dims, preferred_element_type=F32) + lax.dot_general(
        lo, chosen_ref[...], dims, preferred_element_type=F32
    )


def panel_kernel(v_ref, cd_ref, ab_ref, hi_ref, lo_ref):
    for j in range(v_ref.shape[0] // BLOCK):
        cd = down(cd_ref[j : j + 1, :])
        for k in range(v_ref.shape[1] // BLOCK):
            at = (slice(j * BLOCK, (j + 1) * BLOCK), slice(k * BLOCK, (k + 1) * BLOCK))
            v = jnp.where(cd == ab_ref[:, at[1]], v_ref[at], 0.0)
            hi = v.astype(BF16)
            hi_ref[at] = hi
            lo_ref[at] = (v - hi.astype(F32)).astype(BF16)


def product(t, rows, hi_ref, lo_ref):
    t_hi = t.astype(BF16)
    t_lo = (t - t_hi.astype(F32)).astype(BF16)
    total = None
    for a, b in ((t_hi, hi_ref), (t_hi, lo_ref), (t_lo, hi_ref)):
        term = lax.dot_general(a, b[rows, :], (((0,), (0,)), ((), ())), preferred_element_type=F32)
        total = term if total is None else total + term
    return total


def mine_kernel(place_ref, t_ref, hi_ref, lo_ref, out_ref):
    rows = pl.ds(pl.multiple_of(place_ref[0] * CD_CORE, CD_CORE), CD_CORE)
    out_ref[...] = product(t_ref[...], rows, hi_ref, lo_ref)


def other_kernel(place_ref, t_ref, hi_ref, lo_ref, mine_ref, out_ref):
    rows = pl.ds(pl.multiple_of((1 - place_ref[0]) * CD_CORE, CD_CORE), CD_CORE)
    out_ref[...] = mine_ref[...] + product(t_ref[...], rows, hi_ref, lo_ref)


def sum_kernel(x_ref, own_ref, shared_ref):
    total = x_ref[0]
    for b in range(1, BLOCKS):
        total = total + x_ref[b]
    own_ref[...] = total[:OWN]
    shared_ref[...] = total[OWN:]


def spread(a, slots, labels, ab_ref, out_ref):
    chosen = jnp.where(lax.broadcasted_iota(I32, (a.shape[0], BLOCK), 0) == slots, 1.0, 0.0).astype(BF16)
    total = None
    for part in split3(a):
        term = lax.dot_general(chosen, part, (((0,), (0,)), ((), ())), preferred_element_type=F32)
        total = term if total is None else total + term
    ij = down(labels)
    for k in range(out_ref.shape[1] // BLOCK):
        cols = slice(k * BLOCK, (k + 1) * BLOCK)
        out_ref[:, cols] = jnp.where(ij == ab_ref[:, cols], 0.5 * total[:, cols], 0.0)


def first_kernel(place_ref, own_ref, y0_ref, y1_ref, y2_ref, y3_ref, slot_ref, ij_ref, ab_ref, out_ref):
    x, y = place_ref[2], place_ref[3]
    row = 4 * x + y
    slots = slot_ref[pl.ds(row, 1), :]
    block, inner = slots >> 5, slots & (2 * OWN - 1)
    away = (((block >> 2) - x) & 3) * 4 + ((block - y) & 3)
    place = jnp.where(inner < OWN, inner, inner + away * OWN)
    place = jnp.where(slots < SLOTS, place, -1)
    a = jnp.concatenate([own_ref[...], y0_ref[...], y1_ref[...], y2_ref[...], y3_ref[...]], axis=0)
    spread(a, place, ij_ref[pl.ds(row, 1), :], ab_ref, out_ref)


def later_kernel(place_ref, round_ref, a_ref, slot_ref, ij_ref, ab_ref, out_ref):
    row = 4 * place_ref[2] + place_ref[3]
    slots = slot_ref[pl.ds(row, 1), :] - round_ref[0] * SLOTS
    spread(a_ref[...], slots, ij_ref[pl.ds(row, 1), :], ab_ref, out_ref)


def from_next(value, axis, step):
    return lax.ppermute(value, axis, [((i + step) % 4, i) for i in range(4)])


def body(amplitudes, integrals, ij_irrep, cd_irrep, ab_irrep):
    smem = pl.BlockSpec(memory_space=pltpu.SMEM)
    vmem = pl.BlockSpec(memory_space=pltpu.VMEM)
    shape = jax.ShapeDtypeStruct
    place = jnp.stack([lax.axis_index(axis) for axis in ("core", "z", "x", "y")]).astype(I32)
    ij = ij_irrep.reshape(BLOCKS, BLOCK)
    cd = cd_irrep.reshape(-1, BLOCK)
    ab = ab_irrep.reshape(1, -1)
    cds, abs_ = integrals.shape
    row = ("x", "y")

    arrived = lax.all_to_all(amplitudes, ("x", "y", "core"), split_axis=1, concat_axis=0, tiled=True)
    turned = call(turn_kernel, shape((CD_CORE, BLOCK), F32), [smem, vmem, vmem, vmem])(place, arrived, ij, cd)
    line = lax.all_gather(turned, "z", axis=0, tiled=True).reshape(BLOCKS, CD_CORE, BLOCK)

    v_hi, v_lo = call(panel_kernel, [shape((cds, abs_), BF16)] * 2, [vmem] * 3, (2_000_000, 3_200_000))(integrals, cd, ab)

    def tables(number):
        return call(
            table_kernel,
            [shape((BLOCKS, BLOCK), I32), shape((SLOTS, BLOCKS * BLOCK), BF16)],
            [smem, vmem],
            (4_000_000, 2_100_000),
        )(number, ij)

    def products(chosen):
        packed = call(
            pack_kernel,
            shape((CD_CORE, SLOTS), F32),
            [
                pl.BlockSpec((STEP, CD_CORE, BLOCK), lambda i: (i, 0, 0)),
                pl.BlockSpec((SLOTS, STEP * BLOCK), lambda i: (0, i)),
            ],
            (1_600_000_000, 6_000_000),
            grid=(BLOCKS // STEP,),
            out_specs=pl.BlockSpec((CD_CORE, SLOTS), lambda i: (0, 0)),
        )(line, chosen)
        other = lax.ppermute(packed, "core", [(0, 1), (1, 0)])
        cost = (600_000_000, 3_000_000)
        full = shape((SLOTS, abs_), F32)
        mine = call(mine_kernel, full, [smem] + [vmem] * 3, cost)(place, packed, v_hi, v_lo)
        return call(other_kernel, full, [smem] + [vmem] * 4, cost)(place, other, v_hi, v_lo, mine)

    slots, chosen = tables(jnp.zeros((1,), I32))
    partial = lax.all_to_all(products(chosen), row, split_axis=0, concat_axis=0, tiled=True)
    piece = shape((OWN, abs_), F32)
    own, shared = call(sum_kernel, [piece, piece], [vmem])(partial.reshape(BLOCKS, 2 * OWN, abs_))
    along_y = jnp.concatenate([shared] + [from_next(shared, "y", j) for j in (1, 2, 3)], axis=0)
    parts = [along_y] + [from_next(along_y, "x", i) for i in (1, 2, 3)]
    out = call(first_kernel, shape((BLOCK, abs_), F32), [smem] + [vmem] * 8)(place, own, *parts, slots, ij, ab)
    rounds = (jnp.max(slots) >> 9) + 1

    def again(state):
        number, out = state
        _, chosen = tables(number[None])
        whole = lax.psum(products(chosen), row)
        more = call(later_kernel, shape((BLOCK, abs_), F32), [smem] * 2 + [vmem] * 4)(
            place, number[None], whole, slots, ij, ab
        )
        return number + 1, out + more

    return lax.while_loop(lambda state: state[0] < rounds, again, (jnp.int32(1), out))[1]


def solution(mesh):
    finer = Mesh(mesh.devices.reshape(4, 4, 16, 2), ("x", "y", "z", "core"))
    in_specs = (P(("z", "core", "x", "y"), None), P(("x", "y"), ("z", "core")), P(), P(("x", "y")), P(("z", "core")))
    out_specs = P(("x", "y"), ("z", "core"))
    return jax.shard_map(body, mesh=finer, in_specs=in_specs, out_specs=out_specs, check_vma=False)
```

```python
import jax
import jax.numpy as jnp
from jax import lax
from jax.experimental import pallas as pl
from jax.experimental.pallas import tpu as pltpu
from jax.sharding import Mesh
from jax.sharding import PartitionSpec as P

BLOCK = 128
BLOCKS = 16
LABELS = 8
OWN = 16
HALF = BLOCKS * OWN
SLOTS = 2 * HALF
CD_CORE = 384
CD_DEV = 24
F32, BF16, I32 = jnp.float32, jnp.bfloat16, jnp.int32


def call(kernel, out_shape, in_specs=None, cost=(1_000_000, 1_000_000), **kwargs):
    return pl.pallas_call(
        kernel,
        out_shape=out_shape,
        compiler_params=pltpu.CompilerParams(vmem_limit_bytes=48 * 1024 * 1024),
        cost_estimate=pl.CostEstimate(flops=cost[0], bytes_accessed=cost[1], transcendentals=0),
        **({} if in_specs is None else {"in_specs": in_specs}),
        **kwargs,
    )


def split3(x):
    hi = x.astype(BF16)
    rest = x - hi.astype(F32)
    mid = rest.astype(BF16)
    return hi, mid, (rest - mid.astype(F32)).astype(BF16)


def down(row):
    return jnp.transpose(jnp.broadcast_to(row, (BLOCK, BLOCK)))


def arrival(rows):
    n = lax.broadcasted_iota(I32, (BLOCK, BLOCK), 0)
    p = lax.broadcasted_iota(I32, (BLOCK, BLOCK), 1)
    move = n == ((p >> 2) & 1) * 64 + (p >> 3) * 4 + (p & 3)
    return jnp.dot(rows, move.astype(F32), precision=lax.Precision.HIGHEST, preferred_element_type=F32)


def turn_kernel(place_ref, x_ref, ij_ref, cd_ref, chosen_ref, hi_ref, out_ref):
    core, z = place_ref[0], place_ref[1]
    labels = jnp.broadcast_to(ij_ref[pl.ds(z, 1), :], (8, BLOCK)).astype(F32)
    labels = arrival(labels)[0:1, :].astype(I32)
    for j in range(CD_CORE // BLOCK):
        cols = slice(j * BLOCK, (j + 1) * BLOCK)
        cd = down(cd_ref[pl.ds(core * (CD_CORE // BLOCK) + j, 1), :])
        x = x_ref[:, :, cols].reshape(BLOCK, BLOCK)
        out_ref[cols, :] = jnp.where(cd == labels, jnp.transpose(x), 0.0)


def table_kernel(round_ref, ij_ref, slot_ref, chosen_ref):
    ij = ij_ref[...]
    label = lax.broadcasted_iota(I32, (BLOCKS, LABELS, BLOCK), 1)
    same = (jnp.broadcast_to(ij[:, None, :], label.shape) == label).astype(F32)
    upto = lax.broadcasted_iota(I32, (BLOCK, BLOCK), 0) <= lax.broadcasted_iota(I32, (BLOCK, BLOCK), 1)
    count = jnp.dot(
        same.reshape(BLOCKS * LABELS, BLOCK).astype(BF16), upto.astype(BF16), preferred_element_type=F32
    ).reshape(BLOCKS, LABELS, BLOCK)
    excess = jnp.maximum(count[:, :, BLOCK - 1 :] - OWN, 0.0)
    before = jnp.zeros((1, LABELS, 1), F32)
    own_rows, over_rows = [], []
    for b in range(BLOCKS):
        rank = count[b : b + 1] - 1.0
        over = jnp.where(rank < OWN, -1.0, rank - OWN + before)
        own_rows.append(jnp.sum(rank * same[b : b + 1], axis=1) + b * 2 * OWN)
        over_rows.append(jnp.sum(over * same[b : b + 1], axis=1))
        before = before + excess[b : b + 1]
    own = jnp.concatenate(own_rows, axis=0).astype(I32)
    over = jnp.concatenate(over_rows, axis=0).astype(I32)
    shared = (over >> 4) * (2 * OWN) + OWN + (over & (OWN - 1))
    slots = jnp.where(over < 0, own, jnp.where(over < HALF, shared, over + HALF))
    slot_ref[...] = slots
    here = arrival(slots.astype(F32)).astype(I32) - round_ref[0] * SLOTS
    want = lax.broadcasted_iota(I32, (SLOTS, BLOCK), 0)
    for b in range(BLOCKS):
        chosen_ref[:, b * BLOCK : (b + 1) * BLOCK] = jnp.where(want == here[b : b + 1], 1.0, 0.0).astype(BF16)


def pack_kernel(x_ref, chosen_ref, packed_ref):
    total = jnp.zeros((2 * CD_DEV, SLOTS), F32)
    for b in range(0, BLOCKS, 2):
        x = jnp.concatenate([x_ref[b], x_ref[b + 1]], axis=1)
        hi = x.astype(BF16).astype(F32)
        parts = jnp.concatenate([hi, x - hi], axis=0).astype(BF16)
        chosen = chosen_ref[:, b * BLOCK : (b + 2) * BLOCK]
        total += lax.dot_general(parts, chosen, (((1,), (1,)), ((), ())), preferred_element_type=F32)
    packed_ref[...] = total[:CD_DEV] + total[CD_DEV:]


def panel_kernel(v_ref, cd_ref, ab_ref, hi_ref, lo_ref):
    for j in range(v_ref.shape[0] // BLOCK):
        cd = down(cd_ref[j : j + 1, :])
        for k in range(v_ref.shape[1] // BLOCK):
            at = (slice(j * BLOCK, (j + 1) * BLOCK), slice(k * BLOCK, (k + 1) * BLOCK))
            v = jnp.where(cd == ab_ref[:, at[1]], v_ref[at], 0.0)
            hi = v.astype(BF16)
            hi_ref[at] = hi
            lo_ref[at] = (v - hi.astype(F32)).astype(BF16)


def product(t, rows, hi_ref, lo_ref):
    t_hi = t.astype(BF16)
    t_lo = (t - t_hi.astype(F32)).astype(BF16)
    total = None
    for a, b in ((t_hi, hi_ref), (t_hi, lo_ref), (t_lo, hi_ref)):
        term = lax.dot_general(a, b[rows, :], (((0,), (0,)), ((), ())), preferred_element_type=F32)
        total = term if total is None else total + term
    return total


def mine_kernel(place_ref, t_ref, hi_ref, lo_ref, out_ref):
    rows = pl.ds(pl.multiple_of(place_ref[0] * CD_CORE, CD_CORE), CD_CORE)
    out_ref[...] = product(t_ref[...], rows, hi_ref, lo_ref)


def other_kernel(place_ref, t_ref, hi_ref, lo_ref, mine_ref, out_ref):
    rows = pl.ds(pl.multiple_of((1 - place_ref[0]) * CD_CORE, CD_CORE), CD_CORE)
    out_ref[...] = mine_ref[...] + product(t_ref[...], rows, hi_ref, lo_ref)


def sum_kernel(x_ref, own_ref, copies_ref):
    total = x_ref[0]
    for b in range(1, BLOCKS):
        total = total + x_ref[b]
    own_ref[...] = total[:OWN]
    for b in range(BLOCKS):
        copies_ref[b] = total[OWN:]


def spread(a, slots, labels, ab_ref, out_ref):
    chosen = jnp.where(lax.broadcasted_iota(I32, (a.shape[0], BLOCK), 0) == slots, 1.0, 0.0).astype(BF16)
    total = None
    for part in split3(a):
        term = lax.dot_general(chosen, part, (((0,), (0,)), ((), ())), preferred_element_type=F32)
        total = term if total is None else total + term
    ij = down(labels)
    for k in range(out_ref.shape[1] // BLOCK):
        cols = slice(k * BLOCK, (k + 1) * BLOCK)
        out_ref[:, cols] = jnp.where(ij == ab_ref[:, cols], 0.5 * total[:, cols], 0.0)


def first_kernel(place_ref, own_ref, shared_ref, slot_ref, ij_ref, ab_ref, out_ref):
    row = place_ref[2]
    slots = slot_ref[pl.ds(row, 1), :]
    block, inner = slots >> 5, slots & (2 * OWN - 1)
    place = jnp.where(inner < OWN, inner, inner + block * OWN)
    place = jnp.where(slots < SLOTS, place, -1)
    spread(jnp.concatenate([own_ref[...], shared_ref[...]], axis=0), place, ij_ref[pl.ds(row, 1), :], ab_ref, out_ref)


def later_kernel(place_ref, round_ref, a_ref, slot_ref, ij_ref, ab_ref, out_ref):
    row = place_ref[2]
    slots = slot_ref[pl.ds(row, 1), :] - round_ref[0] * SLOTS
    spread(a_ref[...], slots, ij_ref[pl.ds(row, 1), :], ab_ref, out_ref)


def body(amplitudes, integrals, ij_irrep, cd_irrep, ab_irrep):
    smem = pl.BlockSpec(memory_space=pltpu.SMEM)
    vmem = pl.BlockSpec(memory_space=pltpu.VMEM)
    anywhere = pl.BlockSpec(memory_space=pl.ANY)
    shape = jax.ShapeDtypeStruct
    place = jnp.stack([lax.axis_index("core"), lax.axis_index("z"), lax.axis_index("row")]).astype(I32)
    ij = ij_irrep.reshape(BLOCKS, BLOCK)
    cd = cd_irrep.reshape(-1, BLOCK)
    ab = ab_irrep.reshape(1, -1)
    cds, abs_ = integrals.shape

    def tables(number):
        return call(
            table_kernel,
            [shape((BLOCKS, BLOCK), I32), shape((SLOTS, BLOCKS * BLOCK), BF16)],
            [smem, vmem],
            (4_000_000, 2_100_000),
        )(number, ij)

    arrived = lax.all_to_all(
        amplitudes.reshape(4, 2 * BLOCKS, CD_CORE), ("row", "core"), split_axis=1, concat_axis=0, tiled=False
    )
    slots, chosen = tables(jnp.zeros((1,), I32))
    v_hi, v_lo = call(panel_kernel, [shape((cds, abs_), BF16)] * 2, [vmem] * 3, (2_000_000, 3_200_000))(integrals, cd, ab)
    turned = call(turn_kernel, shape((CD_CORE, BLOCK), F32), [smem] + [vmem] * 3 + [anywhere] * 2)(
        place, arrived, ij, cd, chosen, v_hi
    )
    mine = lax.all_to_all(turned, "z", split_axis=0, concat_axis=0, tiled=True).reshape(BLOCKS, CD_DEV, BLOCK)

    def products(chosen):
        packed = call(pack_kernel, shape((CD_DEV, SLOTS), F32), [vmem] * 2)(mine, chosen)
        gathered = lax.all_gather(packed, "z", axis=0, tiled=True)
        other = lax.ppermute(gathered, "core", [(0, 1), (1, 0)])
        cost = (600_000_000, 3_000_000)
        full = shape((SLOTS, abs_), F32)
        half = call(mine_kernel, full, [smem] + [vmem] * 3, cost)(place, gathered, v_hi, v_lo)
        return call(other_kernel, full, [smem] + [vmem] * 4, cost)(place, other, v_hi, v_lo, half)

    partial = lax.all_to_all(products(chosen), "row", split_axis=0, concat_axis=0, tiled=True)
    own, copies = call(sum_kernel, [shape((OWN, abs_), F32), shape((BLOCKS, OWN, abs_), F32)], [vmem])(
        partial.reshape(BLOCKS, 2 * OWN, abs_)
    )
    shared = lax.all_to_all(copies.reshape(HALF, abs_), "row", split_axis=0, concat_axis=0, tiled=True)
    out = call(first_kernel, shape((BLOCK, abs_), F32), [smem] + [vmem] * 5)(place, own, shared, slots, ij, ab)
    rounds = (jnp.max(slots) >> 9) + 1

    def again(state):
        number, out = state
        _, chosen = tables(number[None])
        whole = lax.psum(products(chosen), "row")
        more = call(later_kernel, shape((BLOCK, abs_), F32), [smem] * 2 + [vmem] * 4)(
            place, number[None], whole, slots, ij, ab
        )
        return number + 1, out + more

    return lax.while_loop(lambda state: state[0] < rounds, again, (jnp.int32(1), out))[1]


def solution(mesh):
    finer = Mesh(mesh.devices.reshape(16, 16, 2), ("row", "z", "core"))
    in_specs = (P(("z", "core", "row"), None), P("row", ("z", "core")), P(), P("row"), P(("z", "core")))
    out_specs = P("row", ("z", "core"))
    return jax.shard_map(body, mesh=finer, in_specs=in_specs, out_specs=out_specs, check_vma=False)
```

```python
import jax
import jax.numpy as jnp
from jax import lax
from jax.experimental import pallas as pl
from jax.experimental.pallas import tpu as pltpu
from jax.sharding import Mesh
from jax.sharding import PartitionSpec as P

BLOCK = 128
BLOCKS = 16
LABELS = 8
GROUP = 4
GROUPS = BLOCKS // GROUP
CAP = 160
PART = CAP // 4
SLOTS = GROUPS * CAP
CD_DEV = 96
WIDE = 128
F32, BF16, I32 = jnp.float32, jnp.bfloat16, jnp.int32


def call(kernel, out_shape, in_specs=None, cost=(1_000_000, 1_000_000), **kwargs):
    return pl.pallas_call(
        kernel,
        out_shape=out_shape,
        compiler_params=pltpu.CompilerParams(vmem_limit_bytes=48 * 1024 * 1024),
        cost_estimate=pl.CostEstimate(flops=cost[0], bytes_accessed=cost[1], transcendentals=0),
        **({} if in_specs is None else {"in_specs": in_specs}),
        **kwargs,
    )


def split3(x):
    hi = x.astype(BF16)
    rest = x - hi.astype(F32)
    mid = rest.astype(BF16)
    return hi, mid, (rest - mid.astype(F32)).astype(BF16)


def down(row):
    return jnp.transpose(jnp.broadcast_to(row, (BLOCK, BLOCK)))


def deal_kernel(x_ref, out_ref):
    rows = BLOCKS
    for z in range(GROUP):
        for core in range(2):
            for row in range(rows):
                start = ((row * GROUP + z) * 2 + core) * CD_DEV
                to = (z * 2 + core) * rows + row
                if start + WIDE <= x_ref.shape[1]:
                    out_ref[to] = x_ref[:, start : start + WIDE]
                else:
                    rest = jnp.zeros((x_ref.shape[0], WIDE - CD_DEV), F32)
                    out_ref[to] = jnp.concatenate([x_ref[:, start : start + CD_DEV], rest], axis=1)


def ranks(ij):
    label = lax.broadcasted_iota(I32, (BLOCKS, LABELS, BLOCK), 1)
    same = (jnp.broadcast_to(ij[:, None, :], label.shape) == label).astype(F32)
    upto = lax.broadcasted_iota(I32, (BLOCK, BLOCK), 0) <= lax.broadcasted_iota(I32, (BLOCK, BLOCK), 1)
    count = jnp.dot(
        same.reshape(BLOCKS * LABELS, BLOCK).astype(BF16), upto.astype(BF16), preferred_element_type=F32
    ).reshape(BLOCKS, LABELS, BLOCK)
    rows = []
    for b in range(BLOCKS):
        if b % GROUP == 0:
            before = jnp.zeros((1, LABELS, 1), F32)
        rows.append(jnp.sum((count[b : b + 1] - 1.0 + before) * same[b : b + 1], axis=1))
        before = before + count[b : b + 1, :, BLOCK - 1 :]
    return jnp.concatenate(rows, axis=0).astype(I32)


def table_kernel(place_ref, round_ref, ij_ref, cd_ref, rank_ref, chosen_ref, keep_ref):
    core, z, group = place_ref[0], place_ref[1], place_ref[2]
    rank_ref[...] = ranks(ij_ref[...])
    cd = cd_ref[pl.ds(z * 2 + core, 1), :]
    want = lax.broadcasted_iota(I32, (CAP, BLOCK), 0)
    for b in range(GROUP):
        at = slice(b * BLOCK, (b + 1) * BLOCK)
        here = rank_ref[pl.ds(group * GROUP + b, 1), :] - round_ref[0] * CAP
        chosen_ref[:, at] = jnp.where(want == here, 1.0, 0.0).astype(BF16)
        keep_ref[at, :] = jnp.where(down(ij_ref[pl.ds(group * GROUP + b, 1), :]) == cd, 1.0, 0.0)


def pack_kernel(x_ref, chosen_ref, keep_ref, first_ref, out_ref):
    total = jnp.zeros((CAP, WIDE), F32)
    for b in range(GROUP):
        at = slice(b * BLOCK, (b + 1) * BLOCK)
        x = x_ref[b * 32 : (b + 1) * 32].reshape(BLOCK, WIDE)
        x = jnp.where(keep_ref[at, :] > 0.0, x, 0.0)
        hi = x.astype(BF16)
        lo = (x - hi.astype(F32)).astype(BF16)
        for part in (hi, lo):
            total += jnp.dot(chosen_ref[:, at], part, preferred_element_type=F32)
    lane = lax.broadcasted_iota(I32, (PART, WIDE), 1)
    last = total[3 * PART :]
    for k in range(3):
        at = slice(k * PART, (k + 1) * PART)
        out_ref[at, :] = jnp.where(lane < CD_DEV, total[at], pltpu.roll(last, 96 - 32 * k, 1))


def panel_kernel(v_ref, cd_ref, ab_ref, hi_ref, lo_ref, kept_ref):
    for j in range(v_ref.shape[0] // BLOCK):
        cd = down(cd_ref[j : j + 1, :])
        for k in range(v_ref.shape[1] // BLOCK):
            at = (slice(j * BLOCK, (j + 1) * BLOCK), slice(k * BLOCK, (k + 1) * BLOCK))
            kept_ref[at] = jnp.where(cd == ab_ref[:, at[1]], v_ref[at], 0.0)
    nothing = jnp.zeros((WIDE - CD_DEV, v_ref.shape[1]), BF16)
    for core in range(2):
        for z in range(GROUP):
            start, to = (z * 2 + core) * CD_DEV, (core * GROUP + z) * WIDE
            v = kept_ref[start : start + CD_DEV, :]
            hi = v.astype(BF16)
            hi_ref[to : to + CD_DEV, :] = hi
            lo_ref[to : to + CD_DEV, :] = (v - hi.astype(F32)).astype(BF16)
            hi_ref[to + CD_DEV : to + WIDE, :] = nothing
            lo_ref[to + CD_DEV : to + WIDE, :] = nothing


def unfold(x):
    lane = lax.broadcasted_iota(I32, (PART, WIDE), 1)
    rolled = [pltpu.roll(x[k * PART : (k + 1) * PART], 32 + 32 * k, 1) for k in range(3)]
    last = jnp.where(lane < 32, rolled[0], jnp.where(lane < 64, rolled[1], rolled[2]))
    return jnp.concatenate([x, last], axis=0)


def product(t_ref, core, hi_ref, lo_ref):
    rows = pl.ds(pl.multiple_of(core * GROUP * WIDE, GROUP * WIDE), GROUP * WIDE)
    t = jnp.concatenate(
        [jnp.concatenate([unfold(t_ref[g * GROUP + z]) for z in range(GROUP)], axis=1) for g in range(GROUPS)], axis=0
    )
    t_hi = t.astype(BF16)
    t_lo = (t - t_hi.astype(F32)).astype(BF16)
    total = None
    for a, b in ((t_hi, hi_ref), (t_hi, lo_ref), (t_lo, hi_ref)):
        term = jnp.dot(a, b[rows, :], preferred_element_type=F32)
        total = term if total is None else total + term
    return total


def mine_kernel(place_ref, t_ref, hi_ref, lo_ref, out_ref):
    out_ref[...] = product(t_ref, place_ref[0], hi_ref, lo_ref)


def other_kernel(place_ref, t_ref, hi_ref, lo_ref, mine_ref, out_ref):
    out_ref[...] = mine_ref[...] + product(t_ref, 1 - place_ref[0], hi_ref, lo_ref)


def sum_kernel(x_ref, copies_ref):
    total = x_ref[0]
    for b in range(1, BLOCKS):
        total = total + x_ref[b]
    for b in range(copies_ref.shape[0]):
        copies_ref[b] = total


def spread(a, slots, labels, ab_ref, out_ref):
    chosen = jnp.where(lax.broadcasted_iota(I32, (a.shape[0], BLOCK), 0) == slots, 1.0, 0.0).astype(BF16)
    total = None
    for part in split3(a):
        term = lax.dot_general(chosen, part, (((0,), (0,)), ((), ())), preferred_element_type=F32)
        total = term if total is None else total + term
    ij = down(labels)
    for k in range(out_ref.shape[1] // BLOCK):
        cols = slice(k * BLOCK, (k + 1) * BLOCK)
        out_ref[:, cols] = jnp.where(ij == ab_ref[:, cols], 0.5 * total[:, cols], 0.0)


def expand_kernel(place_ref, round_ref, a_ref, rank_ref, ij_ref, ab_ref, out_ref):
    row = place_ref[3]
    slots = rank_ref[pl.ds(row, 1), :] - round_ref[0] * CAP
    spread(a_ref[...], slots, ij_ref[pl.ds(row, 1), :], ab_ref, out_ref)


def body(amplitudes, integrals, ij_irrep, cd_irrep, ab_irrep):
    smem = pl.BlockSpec(memory_space=pltpu.SMEM)
    vmem = pl.BlockSpec(memory_space=pltpu.VMEM)
    anywhere = pl.BlockSpec(memory_space=pl.ANY)
    shape = jax.ShapeDtypeStruct
    row = ("x", "y")
    place = jnp.stack([lax.axis_index(axis) for axis in ("core", "zl", "zh", row)]).astype(I32)
    ij = ij_irrep.reshape(BLOCKS, BLOCK)
    cd = cd_irrep.reshape(-1, BLOCK)
    cd_own = jnp.pad(cd_irrep.reshape(-1, CD_DEV), ((0, 0), (0, WIDE - CD_DEV)), constant_values=-1)
    ab = ab_irrep.reshape(1, -1)
    cds, abs_ = integrals.shape
    devices = 2 * GROUP * BLOCKS

    dealt = call(deal_kernel, shape((devices, 4, WIDE), F32), [vmem])(amplitudes)
    arrived = lax.all_to_all(dealt, ("zl", "core", "x", "y"), split_axis=0, concat_axis=0, tiled=True)
    v_hi, v_lo = call(
        panel_kernel,
        [shape((2 * GROUP * WIDE, abs_), BF16)] * 2,
        [vmem] * 3,
        (2_000_000, 3_200_000),
        scratch_shapes=[pltpu.VMEM((cds, abs_), F32)],
    )(integrals, cd, ab)

    def tables(number):
        return call(
            table_kernel,
            [shape((BLOCKS, BLOCK), I32), shape((CAP, GROUP * BLOCK), BF16), shape((GROUP * BLOCK, WIDE), F32)],
            [smem, smem, vmem, vmem],
        )(place, number, ij, cd_own)

    def products(chosen, keep):
        packed = call(pack_kernel, shape((3 * PART, WIDE), F32), [vmem] * 3 + [anywhere])(arrived, chosen, keep, v_hi)
        gathered = lax.all_gather(packed, ("zh", "zl"), axis=0, tiled=True)
        other = lax.ppermute(gathered, "core", [(0, 1), (1, 0)])
        pieces = (BLOCKS, 3 * PART, WIDE)
        cost = (1_000_000_000, 3_000_000)
        full = shape((SLOTS, abs_), F32)
        half = call(mine_kernel, full, [smem] + [vmem] * 3, cost)(place, gathered.reshape(pieces), v_hi, v_lo)
        return call(other_kernel, full, [smem] + [vmem] * 4, cost)(place, other.reshape(pieces), v_hi, v_lo, half)

    def expand(number, a):
        return call(expand_kernel, shape((BLOCK, abs_), F32), [smem] * 2 + [vmem] * 4)(place, number, a, rank, ij, ab)

    start = jnp.zeros((1,), I32)
    rank, chosen, keep = tables(start)
    partial = lax.all_to_all(products(chosen, keep), row, split_axis=0, concat_axis=0, tiled=True)
    copies = call(sum_kernel, shape((4, PART, abs_), F32), [vmem])(partial.reshape(BLOCKS, PART, abs_))
    out = expand(start, lax.all_to_all(copies.reshape(CAP, abs_), "y", split_axis=0, concat_axis=0, tiled=True))
    most = jnp.max(rank)

    def again(state):
        number, out = state
        _, chosen, keep = tables(number[None])
        whole = lax.psum(products(chosen, keep), row)
        mine = lax.dynamic_slice_in_dim(whole, lax.axis_index("x") * CAP, CAP, 0)
        return number + 1, out + expand(number[None], mine)

    return lax.while_loop(lambda state: state[0] * CAP <= most, again, (jnp.int32(1), out))[1]


def solution(mesh):
    finer = Mesh(mesh.devices.reshape(4, 4, 4, 4, 2), ("x", "y", "zh", "zl", "core"))
    col = ("zh", "zl", "core")
    in_specs = (P(col + ("x", "y"), None), P(("x", "y"), col), P(), P(("x", "y")), P(col))
    out_specs = P(("x", "y"), col)
    return jax.shard_map(body, mesh=finer, in_specs=in_specs, out_specs=out_specs, check_vma=False)
```

```python
import jax
import jax.numpy as jnp
from jax import lax
from jax.experimental import pallas as pl
from jax.experimental.pallas import tpu as pltpu
from jax.sharding import Mesh
from jax.sharding import PartitionSpec as P

BLOCK = 128
BLOCKS = 16
LABELS = 8
GROUP = 4
GROUPS = BLOCKS // GROUP
CAP = 160
PART = CAP // 4
SLOTS = GROUPS * CAP
CD_DEV = 96
WIDE = 128
F32, BF16, I32 = jnp.float32, jnp.bfloat16, jnp.int32


def call(kernel, out_shape, in_specs=None, cost=(1_000_000, 1_000_000), **kwargs):
    return pl.pallas_call(
        kernel,
        out_shape=out_shape,
        compiler_params=pltpu.CompilerParams(vmem_limit_bytes=48 * 1024 * 1024),
        cost_estimate=pl.CostEstimate(flops=cost[0], bytes_accessed=cost[1], transcendentals=0),
        **({} if in_specs is None else {"in_specs": in_specs}),
        **kwargs,
    )


def split3(x):
    hi = x.astype(BF16)
    rest = x - hi.astype(F32)
    mid = rest.astype(BF16)
    return hi, mid, (rest - mid.astype(F32)).astype(BF16)


def down(row):
    return jnp.transpose(jnp.broadcast_to(row, (BLOCK, BLOCK)))


def deal_kernel(x_ref, out_ref):
    rows = BLOCKS
    for z in range(GROUP):
        for core in range(2):
            for row in range(rows):
                start = ((row * GROUP + z) * 2 + core) * CD_DEV
                to = (z * 2 + core) * rows + row
                if start + WIDE <= x_ref.shape[1]:
                    out_ref[to] = x_ref[:, start : start + WIDE]
                else:
                    rest = jnp.zeros((x_ref.shape[0], WIDE - CD_DEV), F32)
                    out_ref[to] = jnp.concatenate([x_ref[:, start : start + CD_DEV], rest], axis=1)


def ranks(ij):
    label = lax.broadcasted_iota(I32, (BLOCKS, LABELS, BLOCK), 1)
    same = (jnp.broadcast_to(ij[:, None, :], label.shape) == label).astype(F32)
    upto = lax.broadcasted_iota(I32, (BLOCK, BLOCK), 0) <= lax.broadcasted_iota(I32, (BLOCK, BLOCK), 1)
    count = jnp.dot(
        same.reshape(BLOCKS * LABELS, BLOCK).astype(BF16), upto.astype(BF16), preferred_element_type=F32
    ).reshape(BLOCKS, LABELS, BLOCK)
    rows = []
    for b in range(BLOCKS):
        if b % GROUP == 0:
            before = jnp.zeros((1, LABELS, 1), F32)
        rows.append(jnp.sum((count[b : b + 1] - 1.0 + before) * same[b : b + 1], axis=1))
        before = before + count[b : b + 1, :, BLOCK - 1 :]
    return jnp.concatenate(rows, axis=0).astype(I32)


def table_kernel(place_ref, round_ref, ij_ref, cd_ref, rank_ref, chosen_ref, keep_ref):
    core, z, group = place_ref[0], place_ref[1], place_ref[2]
    rank_ref[...] = ranks(ij_ref[...])
    cd = cd_ref[pl.ds(z * 2 + core, 1), :]
    want = lax.broadcasted_iota(I32, (CAP, BLOCK), 0)
    for b in range(GROUP):
        at = slice(b * BLOCK, (b + 1) * BLOCK)
        here = rank_ref[pl.ds(group * GROUP + b, 1), :] - round_ref[0] * CAP
        chosen_ref[:, at] = jnp.where(want == here, 1.0, 0.0).astype(BF16)
        keep_ref[at, :] = jnp.where(down(ij_ref[pl.ds(group * GROUP + b, 1), :]) == cd, 1.0, 0.0)


def pack_kernel(x_ref, chosen_ref, keep_ref, first_ref, out_ref):
    total = jnp.zeros((CAP, WIDE), F32)
    for b in range(GROUP):
        at = slice(b * BLOCK, (b + 1) * BLOCK)
        x = x_ref[b * 32 : (b + 1) * 32].reshape(BLOCK, WIDE)
        x = jnp.where(keep_ref[at, :] > 0.0, x, 0.0)
        hi = x.astype(BF16)
        lo = (x - hi.astype(F32)).astype(BF16)
        for part in (hi, lo):
            total += jnp.dot(chosen_ref[:, at], part, preferred_element_type=F32)
    lane = lax.broadcasted_iota(I32, (PART, WIDE), 1)
    last = total[3 * PART :]
    for k in range(3):
        at = slice(k * PART, (k + 1) * PART)
        out_ref[at, :] = jnp.where(lane < CD_DEV, total[at], pltpu.roll(last, 96 - 32 * k, 1))


def panel_kernel(v_ref, cd_ref, ab_ref, hi_ref, lo_ref, kept_ref):
    for j in range(v_ref.shape[0] // BLOCK):
        cd = down(cd_ref[j : j + 1, :])
        for k in range(v_ref.shape[1] // BLOCK):
            at = (slice(j * BLOCK, (j + 1) * BLOCK), slice(k * BLOCK, (k + 1) * BLOCK))
            kept_ref[at] = jnp.where(cd == ab_ref[:, at[1]], v_ref[at], 0.0)
    nothing = jnp.zeros((WIDE - CD_DEV, v_ref.shape[1]), BF16)
    for core in range(2):
        for z in range(GROUP):
            start, to = (z * 2 + core) * CD_DEV, (core * GROUP + z) * WIDE
            v = kept_ref[start : start + CD_DEV, :]
            hi = v.astype(BF16)
            hi_ref[to : to + CD_DEV, :] = hi
            lo_ref[to : to + CD_DEV, :] = (v - hi.astype(F32)).astype(BF16)
            hi_ref[to + CD_DEV : to + WIDE, :] = nothing
            lo_ref[to + CD_DEV : to + WIDE, :] = nothing


def unfold(x):
    lane = lax.broadcasted_iota(I32, (PART, WIDE), 1)
    rolled = [pltpu.roll(x[k * PART : (k + 1) * PART], 32 + 32 * k, 1) for k in range(3)]
    last = jnp.where(lane < 32, rolled[0], jnp.where(lane < 64, rolled[1], rolled[2]))
    return jnp.concatenate([x, last], axis=0)


def product(t_ref, core, hi_ref, lo_ref):
    rows = pl.ds(pl.multiple_of(core * GROUP * WIDE, GROUP * WIDE), GROUP * WIDE)
    t = jnp.concatenate(
        [jnp.concatenate([unfold(t_ref[g * GROUP + z]) for z in range(GROUP)], axis=1) for g in range(GROUPS)], axis=0
    )
    t_hi = t.astype(BF16)
    t_lo = (t - t_hi.astype(F32)).astype(BF16)
    total = None
    for a, b in ((t_hi, hi_ref), (t_hi, lo_ref), (t_lo, hi_ref)):
        term = jnp.dot(a, b[rows, :], preferred_element_type=F32)
        total = term if total is None else total + term
    return total


def mine_kernel(place_ref, t_ref, hi_ref, lo_ref, out_ref):
    out_ref[...] = product(t_ref, place_ref[0], hi_ref, lo_ref)


def other_kernel(place_ref, t_ref, hi_ref, lo_ref, mine_ref, out_ref):
    out_ref[...] = mine_ref[...] + product(t_ref, 1 - place_ref[0], hi_ref, lo_ref)


def sum_kernel(x_ref, out_ref):
    total = x_ref[0]
    for b in range(1, BLOCKS):
        total = total + x_ref[b]
    out_ref[...] = total


def spread(a, slots, labels, ab_ref, out_ref):
    chosen = jnp.where(lax.broadcasted_iota(I32, (a.shape[0], BLOCK), 0) == slots, 1.0, 0.0).astype(BF16)
    total = None
    for part in split3(a):
        term = lax.dot_general(chosen, part, (((0,), (0,)), ((), ())), preferred_element_type=F32)
        total = term if total is None else total + term
    ij = down(labels)
    for k in range(out_ref.shape[1] // BLOCK):
        cols = slice(k * BLOCK, (k + 1) * BLOCK)
        out_ref[:, cols] = jnp.where(ij == ab_ref[:, cols], 0.5 * total[:, cols], 0.0)


def expand_kernel(place_ref, round_ref, a_ref, rank_ref, ij_ref, ab_ref, out_ref):
    row = place_ref[3]
    slots = rank_ref[pl.ds(row, 1), :] - round_ref[0] * CAP
    spread(a_ref[...], slots, ij_ref[pl.ds(row, 1), :], ab_ref, out_ref)


def body(amplitudes, integrals, ij_irrep, cd_irrep, ab_irrep):
    smem = pl.BlockSpec(memory_space=pltpu.SMEM)
    vmem = pl.BlockSpec(memory_space=pltpu.VMEM)
    anywhere = pl.BlockSpec(memory_space=pl.ANY)
    shape = jax.ShapeDtypeStruct
    row = ("x", "y")
    place = jnp.stack([lax.axis_index(axis) for axis in ("core", "zl", "zh", row)]).astype(I32)
    ij = ij_irrep.reshape(BLOCKS, BLOCK)
    cd = cd_irrep.reshape(-1, BLOCK)
    cd_own = jnp.pad(cd_irrep.reshape(-1, CD_DEV), ((0, 0), (0, WIDE - CD_DEV)), constant_values=-1)
    ab = ab_irrep.reshape(1, -1)
    cds, abs_ = integrals.shape
    devices = 2 * GROUP * BLOCKS

    dealt = call(deal_kernel, shape((devices, 4, WIDE), F32), [vmem])(amplitudes)
    arrived = lax.all_to_all(dealt, ("zl", "core", "x", "y"), split_axis=0, concat_axis=0, tiled=True)
    v_hi, v_lo = call(
        panel_kernel,
        [shape((2 * GROUP * WIDE, abs_), BF16)] * 2,
        [vmem] * 3,
        (2_000_000, 3_200_000),
        scratch_shapes=[pltpu.VMEM((cds, abs_), F32)],
    )(integrals, cd, ab)

    def tables(number):
        return call(
            table_kernel,
            [shape((BLOCKS, BLOCK), I32), shape((CAP, GROUP * BLOCK), BF16), shape((GROUP * BLOCK, WIDE), F32)],
            [smem, smem, vmem, vmem],
        )(place, number, ij, cd_own)

    def products(chosen, keep):
        packed = call(pack_kernel, shape((3 * PART, WIDE), F32), [vmem] * 3 + [anywhere])(arrived, chosen, keep, v_hi)
        gathered = lax.all_gather(packed, ("zh", "zl"), axis=0, tiled=True)
        other = lax.ppermute(gathered, "core", [(0, 1), (1, 0)])
        pieces = (BLOCKS, 3 * PART, WIDE)
        cost = (1_000_000_000, 3_000_000)
        full = shape((SLOTS, abs_), F32)
        half = call(mine_kernel, full, [smem] + [vmem] * 3, cost)(place, gathered.reshape(pieces), v_hi, v_lo)
        return call(other_kernel, full, [smem] + [vmem] * 4, cost)(place, other.reshape(pieces), v_hi, v_lo, half)

    def one_round(number, rank, chosen, keep):
        partial = lax.all_to_all(products(chosen, keep), row, split_axis=0, concat_axis=0, tiled=True)
        summed = call(sum_kernel, shape((PART, abs_), F32), [vmem])(partial.reshape(BLOCKS, PART, abs_))
        summed = lax.all_gather(summed, "y", axis=0, tiled=True)
        return call(expand_kernel, shape((BLOCK, abs_), F32), [smem] * 2 + [vmem] * 4)(
            place, number, summed, rank, ij, ab
        )

    start = jnp.zeros((1,), I32)
    rank, chosen, keep = tables(start)
    out = one_round(start, rank, chosen, keep)
    most = jnp.max(rank)

    def again(state):
        number, out = state
        return number + 1, out + one_round(number[None], *tables(number[None]))

    return lax.while_loop(lambda state: state[0] * CAP <= most, again, (jnp.int32(1), out))[1]


def solution(mesh):
    finer = Mesh(mesh.devices.reshape(4, 4, 4, 4, 2), ("x", "y", "zh", "zl", "core"))
    col = ("zh", "zl", "core")
    in_specs = (P(col + ("x", "y"), None), P(("x", "y"), col), P(), P(("x", "y")), P(col))
    out_specs = P(("x", "y"), col)
    return jax.shard_map(body, mesh=finer, in_specs=in_specs, out_specs=out_specs, check_vma=False)
```

```python
import jax
import jax.numpy as jnp
from jax import lax
from jax.experimental import pallas as pl
from jax.experimental.pallas import tpu as pltpu
from jax.sharding import Mesh
from jax.sharding import PartitionSpec as P

BLOCK = 128
BLOCKS = 16
LABELS = 8
GROUP = 4
GROUPS = BLOCKS // GROUP
CAP = 160
PART = CAP // 4
SLOTS = GROUPS * CAP
CD_DEV = 96
WIDE = 128
F32, BF16, I32 = jnp.float32, jnp.bfloat16, jnp.int32


def call(kernel, out_shape, in_specs=None, cost=(1_000_000, 1_000_000), **kwargs):
    return pl.pallas_call(
        kernel,
        out_shape=out_shape,
        compiler_params=pltpu.CompilerParams(vmem_limit_bytes=48 * 1024 * 1024),
        cost_estimate=pl.CostEstimate(flops=cost[0], bytes_accessed=cost[1], transcendentals=0),
        **({} if in_specs is None else {"in_specs": in_specs}),
        **kwargs,
    )


def split3(x):
    hi = x.astype(BF16)
    rest = x - hi.astype(F32)
    mid = rest.astype(BF16)
    return hi, mid, (rest - mid.astype(F32)).astype(BF16)


def down(row):
    return jnp.transpose(jnp.broadcast_to(row, (BLOCK, BLOCK)))


def deal_kernel(x_ref, out_ref):
    rows = BLOCKS
    for z in range(GROUP):
        for core in range(2):
            for row in range(rows):
                start = ((row * GROUP + z) * 2 + core) * CD_DEV
                to = (z * 2 + core) * rows + row
                if start + WIDE <= x_ref.shape[1]:
                    out_ref[to] = x_ref[:, start : start + WIDE]
                else:
                    rest = jnp.zeros((x_ref.shape[0], WIDE - CD_DEV), F32)
                    out_ref[to] = jnp.concatenate([x_ref[:, start : start + CD_DEV], rest], axis=1)


def ranks(ij):
    label = lax.broadcasted_iota(I32, (BLOCKS, LABELS, BLOCK), 1)
    same = (jnp.broadcast_to(ij[:, None, :], label.shape) == label).astype(F32)
    upto = lax.broadcasted_iota(I32, (BLOCK, BLOCK), 0) <= lax.broadcasted_iota(I32, (BLOCK, BLOCK), 1)
    count = jnp.dot(
        same.reshape(BLOCKS * LABELS, BLOCK).astype(BF16), upto.astype(BF16), preferred_element_type=F32
    ).reshape(BLOCKS, LABELS, BLOCK)
    rows = []
    for b in range(BLOCKS):
        if b % GROUP == 0:
            before = jnp.zeros((1, LABELS, 1), F32)
        rows.append(jnp.sum((count[b : b + 1] - 1.0 + before) * same[b : b + 1], axis=1))
        before = before + count[b : b + 1, :, BLOCK - 1 :]
    return jnp.concatenate(rows, axis=0)


def table_kernel(place_ref, round_ref, ij_ref, cd_ref, most_ref, rank_ref, chosen_ref, keep_ref):
    core, z, group = place_ref[0], place_ref[1], place_ref[2]
    rank = ranks(ij_ref[...])
    most_ref[0] = jnp.max(rank).astype(I32)
    rank_ref[...] = rank.astype(I32)
    cd = cd_ref[pl.ds(z * 2 + core, 1), :]
    want = lax.broadcasted_iota(I32, (CAP, BLOCK), 0)
    for b in range(GROUP):
        at = slice(b * BLOCK, (b + 1) * BLOCK)
        here = rank_ref[pl.ds(group * GROUP + b, 1), :] - round_ref[0] * CAP
        chosen_ref[:, at] = jnp.where(want == here, 1.0, 0.0).astype(BF16)
        keep_ref[at, :] = jnp.where(down(ij_ref[pl.ds(group * GROUP + b, 1), :]) == cd, 1.0, 0.0)


def pack_kernel(x_ref, chosen_ref, keep_ref, first_ref, out_ref):
    total = jnp.zeros((CAP, WIDE), F32)
    for b in range(GROUP):
        at = slice(b * BLOCK, (b + 1) * BLOCK)
        x = x_ref[b * 32 : (b + 1) * 32].reshape(BLOCK, WIDE)
        x = jnp.where(keep_ref[at, :] > 0.0, x, 0.0)
        hi = x.astype(BF16)
        lo = (x - hi.astype(F32)).astype(BF16)
        for part in (hi, lo):
            total += jnp.dot(chosen_ref[:, at], part, preferred_element_type=F32)
    lane = lax.broadcasted_iota(I32, (PART, WIDE), 1)
    last = total[3 * PART :]
    for k in range(3):
        at = slice(k * PART, (k + 1) * PART)
        out_ref[at, :] = jnp.where(lane < CD_DEV, total[at], pltpu.roll(last, 96 - 32 * k, 1))


def panel_kernel(v_ref, cd_ref, ab_ref, hi_ref, lo_ref, kept_ref):
    for j in range(v_ref.shape[0] // BLOCK):
        cd = down(cd_ref[j : j + 1, :])
        for k in range(v_ref.shape[1] // BLOCK):
            at = (slice(j * BLOCK, (j + 1) * BLOCK), slice(k * BLOCK, (k + 1) * BLOCK))
            kept_ref[at] = jnp.where(cd == ab_ref[:, at[1]], v_ref[at], 0.0)
    nothing = jnp.zeros((WIDE - CD_DEV, v_ref.shape[1]), BF16)
    for core in range(2):
        for z in range(GROUP):
            start, to = (z * 2 + core) * CD_DEV, (core * GROUP + z) * WIDE
            v = kept_ref[start : start + CD_DEV, :]
            hi = v.astype(BF16)
            hi_ref[to : to + CD_DEV, :] = hi
            lo_ref[to : to + CD_DEV, :] = (v - hi.astype(F32)).astype(BF16)
            hi_ref[to + CD_DEV : to + WIDE, :] = nothing
            lo_ref[to + CD_DEV : to + WIDE, :] = nothing


def unfold(x):
    lane = lax.broadcasted_iota(I32, (PART, WIDE), 1)
    rolled = [pltpu.roll(x[k * PART : (k + 1) * PART], 32 + 32 * k, 1) for k in range(3)]
    last = jnp.where(lane < 32, rolled[0], jnp.where(lane < 64, rolled[1], rolled[2]))
    return jnp.concatenate([x, last], axis=0)


def product(t_ref, core, hi_ref, lo_ref):
    rows = pl.ds(pl.multiple_of(core * GROUP * WIDE, GROUP * WIDE), GROUP * WIDE)
    t = jnp.concatenate(
        [jnp.concatenate([unfold(t_ref[g * GROUP + z]) for z in range(GROUP)], axis=1) for g in range(GROUPS)], axis=0
    )
    t_hi = t.astype(BF16)
    t_lo = (t - t_hi.astype(F32)).astype(BF16)
    total = None
    for a, b in ((t_hi, hi_ref), (t_hi, lo_ref), (t_lo, hi_ref)):
        term = jnp.dot(a, b[rows, :], preferred_element_type=F32)
        total = term if total is None else total + term
    return total


def mine_kernel(place_ref, t_ref, hi_ref, lo_ref, out_ref):
    out_ref[...] = product(t_ref, place_ref[0], hi_ref, lo_ref)


def other_kernel(place_ref, t_ref, hi_ref, lo_ref, mine_ref, out_ref):
    out_ref[...] = mine_ref[...] + product(t_ref, 1 - place_ref[0], hi_ref, lo_ref)


def sum_kernel(x_ref, copies_ref):
    total = x_ref[0]
    for b in range(1, BLOCKS):
        total = total + x_ref[b]
    for b in range(copies_ref.shape[0]):
        copies_ref[b] = total


def spread(a, slots, labels, ab_ref, out_ref):
    chosen = jnp.where(lax.broadcasted_iota(I32, (a.shape[0], BLOCK), 0) == slots, 1.0, 0.0).astype(BF16)
    total = None
    for part in split3(a):
        term = lax.dot_general(chosen, part, (((0,), (0,)), ((), ())), preferred_element_type=F32)
        total = term if total is None else total + term
    ij = down(labels)
    for k in range(out_ref.shape[1] // BLOCK):
        cols = slice(k * BLOCK, (k + 1) * BLOCK)
        out_ref[:, cols] = jnp.where(ij == ab_ref[:, cols], 0.5 * total[:, cols], 0.0)


def expand_kernel(place_ref, round_ref, a_ref, rank_ref, ij_ref, ab_ref, out_ref):
    row = place_ref[3]
    slots = rank_ref[pl.ds(row, 1), :] - round_ref[0] * CAP
    spread(a_ref[...], slots, ij_ref[pl.ds(row, 1), :], ab_ref, out_ref)


def body(amplitudes, integrals, ij_irrep, cd_irrep, ab_irrep):
    smem = pl.BlockSpec(memory_space=pltpu.SMEM)
    vmem = pl.BlockSpec(memory_space=pltpu.VMEM)
    anywhere = pl.BlockSpec(memory_space=pl.ANY)
    shape = jax.ShapeDtypeStruct
    row = ("x", "y")
    place = jnp.stack([lax.axis_index(axis) for axis in ("core", "zl", "zh", row)]).astype(I32)
    ij = ij_irrep.reshape(BLOCKS, BLOCK)
    cd = cd_irrep.reshape(-1, BLOCK)
    cd_own = jnp.pad(cd_irrep.reshape(-1, CD_DEV), ((0, 0), (0, WIDE - CD_DEV)), constant_values=-1)
    ab = ab_irrep.reshape(1, -1)
    cds, abs_ = integrals.shape
    devices = 2 * GROUP * BLOCKS

    dealt = call(deal_kernel, shape((devices, 4, WIDE), F32), [vmem])(amplitudes)
    arrived = lax.all_to_all(dealt, ("zl", "core", "x", "y"), split_axis=0, concat_axis=0, tiled=True)
    v_hi, v_lo = call(
        panel_kernel,
        [shape((2 * GROUP * WIDE, abs_), BF16)] * 2,
        [vmem] * 3,
        (2_000_000, 3_200_000),
        scratch_shapes=[pltpu.VMEM((cds, abs_), F32)],
    )(integrals, cd, ab)

    def tables(number):
        return call(
            table_kernel,
            [
                shape((1,), I32),
                shape((BLOCKS, BLOCK), I32),
                shape((CAP, GROUP * BLOCK), BF16),
                shape((GROUP * BLOCK, WIDE), F32),
            ],
            [smem, smem, vmem, vmem],
            out_specs=[smem, vmem, vmem, vmem],
        )(place, number, ij, cd_own)

    def products(chosen, keep):
        packed = call(pack_kernel, shape((3 * PART, WIDE), F32), [vmem] * 3 + [anywhere])(arrived, chosen, keep, v_hi)
        gathered = lax.all_gather(packed, ("zh", "zl"), axis=0, tiled=True)
        other = lax.ppermute(gathered, "core", [(0, 1), (1, 0)])
        pieces = (BLOCKS, 3 * PART, WIDE)
        cost = (1_000_000_000, 3_000_000)
        full = shape((SLOTS, abs_), F32)
        half = call(mine_kernel, full, [smem] + [vmem] * 3, cost)(place, gathered.reshape(pieces), v_hi, v_lo)
        return call(other_kernel, full, [smem] + [vmem] * 4, cost)(place, other.reshape(pieces), v_hi, v_lo, half)

    def one_round(number, rank, chosen, keep):
        partial = lax.all_to_all(products(chosen, keep), row, split_axis=0, concat_axis=0, tiled=True)
        copies = call(sum_kernel, shape((4, PART, abs_), F32), [vmem])(partial.reshape(BLOCKS, PART, abs_))
        summed = lax.all_to_all(copies.reshape(CAP, abs_), "y", split_axis=0, concat_axis=0, tiled=True)
        return call(expand_kernel, shape((BLOCK, abs_), F32), [smem] * 2 + [vmem] * 4)(
            place, number, summed, rank, ij, ab
        )

    start = jnp.zeros((1,), I32)
    most, rank, chosen, keep = tables(start)
    out = one_round(start, rank, chosen, keep)

    def again(state):
        number, out = state
        return number + 1, out + one_round(number[None], *tables(number[None])[1:])

    return lax.while_loop(lambda state: state[0] * CAP <= most[0], again, (jnp.int32(1), out))[1]


def solution(mesh):
    finer = Mesh(mesh.devices.reshape(4, 4, 4, 4, 2), ("x", "y", "zh", "zl", "core"))
    col = ("zh", "zl", "core")
    in_specs = (P(col + ("x", "y"), None), P(("x", "y"), col), P(), P(("x", "y")), P(col))
    out_specs = P(("x", "y"), col)
    return jax.shard_map(body, mesh=finer, in_specs=in_specs, out_specs=out_specs, check_vma=False)
```

```python
import jax
import jax.numpy as jnp
from jax import lax
from jax.experimental import pallas as pl
from jax.experimental.pallas import tpu as pltpu
from jax.sharding import Mesh
from jax.sharding import PartitionSpec as P

BLOCK = 128
BLOCKS = 16
LABELS = 8
GROUP = 4
GROUPS = BLOCKS // GROUP
CAP = 160
PART = CAP // 4
SLOTS = GROUPS * CAP
CD_DEV = 96
WIDE = 128
F32, BF16, I32 = jnp.float32, jnp.bfloat16, jnp.int32


def call(kernel, out_shape, in_specs=None, cost=(1_000_000, 1_000_000), vmem_limit=48 * 1024 * 1024, **kwargs):
    return pl.pallas_call(
        kernel,
        out_shape=out_shape,
        compiler_params=pltpu.CompilerParams(vmem_limit_bytes=vmem_limit),
        cost_estimate=pl.CostEstimate(flops=cost[0], bytes_accessed=cost[1], transcendentals=0),
        **({} if in_specs is None else {"in_specs": in_specs}),
        **kwargs,
    )


def split3(x):
    hi = x.astype(BF16)
    rest = x - hi.astype(F32)
    mid = rest.astype(BF16)
    return hi, mid, (rest - mid.astype(F32)).astype(BF16)


def down(row):
    return jnp.transpose(jnp.broadcast_to(row, (BLOCK, BLOCK)))


def deal_kernel(x_ref, out_ref, held_ref, done_ref):
    pieces = 4
    width = x_ref.shape[1] // pieces
    copies = []
    for k in range(pieces):
        cols = slice(k * width, (k + 1) * width)
        copies.append(pltpu.make_async_copy(x_ref.at[:, cols], held_ref.at[:, cols], done_ref.at[k]))
        copies[-1].start()
    rest = jnp.zeros((x_ref.shape[0], WIDE - CD_DEV), F32)
    for k in range(pieces):
        copies[k].wait()
        for row in range(k * BLOCKS // pieces, (k + 1) * BLOCKS // pieces):
            for z in range(GROUP):
                for core in range(2):
                    start = ((row * GROUP + z) * 2 + core) * CD_DEV
                    to = (z * 2 + core) * BLOCKS + row
                    if start + WIDE <= (k + 1) * width:
                        out_ref[to] = held_ref[:, start : start + WIDE]
                    else:
                        out_ref[to] = jnp.concatenate([held_ref[:, start : start + CD_DEV], rest], axis=1)


def ranks(ij):
    label = lax.broadcasted_iota(I32, (BLOCKS, LABELS, BLOCK), 1)
    same = (jnp.broadcast_to(ij[:, None, :], label.shape) == label).astype(F32)
    upto = lax.broadcasted_iota(I32, (BLOCK, BLOCK), 0) <= lax.broadcasted_iota(I32, (BLOCK, BLOCK), 1)
    count = jnp.dot(
        same.reshape(BLOCKS * LABELS, BLOCK).astype(BF16), upto.astype(BF16), preferred_element_type=F32
    ).reshape(BLOCKS, LABELS, BLOCK)
    rows = []
    for b in range(BLOCKS):
        if b % GROUP == 0:
            before = jnp.zeros((1, LABELS, 1), F32)
        rows.append(jnp.sum((count[b : b + 1] - 1.0 + before) * same[b : b + 1], axis=1))
        before = before + count[b : b + 1, :, BLOCK - 1 :]
    return jnp.concatenate(rows, axis=0)


def table_kernel(place_ref, round_ref, ij_ref, cd_ref, most_ref, rank_ref, chosen_ref, keep_ref):
    core, z, group = place_ref[0], place_ref[1], place_ref[2]
    rank = ranks(ij_ref[...])
    most_ref[0] = jnp.max(rank).astype(I32)
    rank_ref[...] = rank.astype(I32)
    cd = cd_ref[pl.ds(z * 2 + core, 1), :]
    want = lax.broadcasted_iota(I32, (CAP, BLOCK), 0)
    for b in range(GROUP):
        at = slice(b * BLOCK, (b + 1) * BLOCK)
        here = rank_ref[pl.ds(group * GROUP + b, 1), :] - round_ref[0] * CAP
        chosen_ref[:, at] = jnp.where(want == here, 1.0, 0.0).astype(BF16)
        keep_ref[at, :] = jnp.where(down(ij_ref[pl.ds(group * GROUP + b, 1), :]) == cd, 1.0, 0.0)


def pack_kernel(x_ref, chosen_ref, keep_ref, first_ref, out_ref):
    total = jnp.zeros((CAP, WIDE), F32)
    for b in range(GROUP):
        at = slice(b * BLOCK, (b + 1) * BLOCK)
        x = x_ref[b * 32 : (b + 1) * 32].reshape(BLOCK, WIDE)
        x = jnp.where(keep_ref[at, :] > 0.0, x, 0.0)
        hi = x.astype(BF16)
        lo = (x - hi.astype(F32)).astype(BF16)
        for part in (hi, lo):
            total += jnp.dot(chosen_ref[:, at], part, preferred_element_type=F32)
    lane = lax.broadcasted_iota(I32, (PART, WIDE), 1)
    last = total[3 * PART :]
    for k in range(3):
        at = slice(k * PART, (k + 1) * PART)
        out_ref[at, :] = jnp.where(lane < CD_DEV, total[at], pltpu.roll(last, 96 - 32 * k, 1))


def panel_kernel(v_ref, cd_ref, ab_ref, out_ref, kept_ref):
    for j in range(v_ref.shape[0] // BLOCK):
        cd = down(cd_ref[j : j + 1, :])
        for k in range(v_ref.shape[1] // BLOCK):
            at = (slice(j * BLOCK, (j + 1) * BLOCK), slice(k * BLOCK, (k + 1) * BLOCK))
            kept_ref[at] = jnp.where(cd == ab_ref[:, at[1]], v_ref[at], 0.0)
    nothing = jnp.zeros((WIDE - CD_DEV, v_ref.shape[1]), BF16)
    for core in range(2):
        for z in range(GROUP):
            start = (z * 2 + core) * CD_DEV
            v = kept_ref[start : start + CD_DEV, :]
            hi = v.astype(BF16)
            lo = (v - hi.astype(F32)).astype(BF16)
            for k, part in enumerate((hi, lo, hi)):
                to = ((core * 3 + k) * GROUP + z) * WIDE
                out_ref[to : to + CD_DEV, :] = part
                out_ref[to + CD_DEV : to + WIDE, :] = nothing


def unfold(x):
    lane = lax.broadcasted_iota(I32, (PART, WIDE), 1)
    rolled = [pltpu.roll(x[k * PART : (k + 1) * PART], 32 + 32 * k, 1) for k in range(3)]
    last = jnp.where(lane < 32, rolled[0], jnp.where(lane < 64, rolled[1], rolled[2]))
    return jnp.concatenate([x, last], axis=0)


def product(t_ref, core, v_ref):
    depth = 3 * GROUP * WIDE
    rows = pl.ds(pl.multiple_of(core * depth, depth), depth)
    t = jnp.concatenate(
        [jnp.concatenate([unfold(t_ref[g * GROUP + z]) for z in range(GROUP)], axis=1) for g in range(GROUPS)], axis=0
    )
    hi = t.astype(BF16)
    lo = (t - hi.astype(F32)).astype(BF16)
    return jnp.dot(jnp.concatenate([hi, hi, lo], axis=1), v_ref[rows, :], preferred_element_type=F32)


def mine_kernel(place_ref, t_ref, v_ref, out_ref):
    out_ref[...] = product(t_ref, place_ref[0], v_ref)


def other_kernel(place_ref, t_ref, v_ref, mine_ref, out_ref):
    out_ref[...] = mine_ref[...] + product(t_ref, 1 - place_ref[0], v_ref)


def sum_kernel(x_ref, copies_ref):
    total = x_ref[0]
    for b in range(1, BLOCKS):
        total = total + x_ref[b]
    for b in range(copies_ref.shape[0]):
        copies_ref[b] = total


def spread(a, slots, labels, ab_ref, out_ref):
    chosen = jnp.where(lax.broadcasted_iota(I32, (a.shape[0], BLOCK), 0) == slots, 1.0, 0.0).astype(BF16)
    total = None
    for part in split3(a):
        term = lax.dot_general(chosen, part, (((0,), (0,)), ((), ())), preferred_element_type=F32)
        total = term if total is None else total + term
    ij = down(labels)
    for k in range(out_ref.shape[1] // BLOCK):
        cols = slice(k * BLOCK, (k + 1) * BLOCK)
        out_ref[:, cols] = jnp.where(ij == ab_ref[:, cols], 0.5 * total[:, cols], 0.0)


def expand_kernel(place_ref, round_ref, a_ref, rank_ref, ij_ref, ab_ref, out_ref):
    row = place_ref[3]
    slots = rank_ref[pl.ds(row, 1), :] - round_ref[0] * CAP
    spread(a_ref[...], slots, ij_ref[pl.ds(row, 1), :], ab_ref, out_ref)


def body(amplitudes, integrals, ij_irrep, cd_irrep, ab_irrep):
    smem = pl.BlockSpec(memory_space=pltpu.SMEM)
    vmem = pl.BlockSpec(memory_space=pltpu.VMEM)
    anywhere = pl.BlockSpec(memory_space=pl.ANY)
    shape = jax.ShapeDtypeStruct
    row = ("x", "y")
    place = jnp.stack([lax.axis_index(axis) for axis in ("core", "zl", "zh", row)]).astype(I32)
    ij = ij_irrep.reshape(BLOCKS, BLOCK)
    cd = cd_irrep.reshape(-1, BLOCK)
    cd_own = jnp.pad(cd_irrep.reshape(-1, CD_DEV), ((0, 0), (0, WIDE - CD_DEV)), constant_values=-1)
    ab = ab_irrep.reshape(1, -1)
    cds, abs_ = integrals.shape
    devices = 2 * GROUP * BLOCKS

    dealt = call(
        deal_kernel,
        shape((devices, 4, WIDE), F32),
        [pl.BlockSpec(memory_space=pltpu.HBM)],
        vmem_limit=None,
        scratch_shapes=[pltpu.VMEM(amplitudes.shape, F32), pltpu.SemaphoreType.DMA((4,))],
    )(amplitudes)
    arrived = lax.all_to_all(dealt, ("zl", "core", "x", "y"), split_axis=0, concat_axis=0, tiled=True)
    panel = call(
        panel_kernel,
        shape((6 * GROUP * WIDE, abs_), BF16),
        [vmem] * 3,
        (2_000_000, 3_200_000),
        scratch_shapes=[pltpu.VMEM((cds, abs_), F32)],
    )(integrals, cd, ab)

    def tables(number):
        return call(
            table_kernel,
            [
                shape((1,), I32),
                shape((BLOCKS, BLOCK), I32),
                shape((CAP, GROUP * BLOCK), BF16),
                shape((GROUP * BLOCK, WIDE), F32),
            ],
            [smem, smem, vmem, vmem],
            out_specs=[smem, vmem, vmem, vmem],
        )(place, number, ij, cd_own)

    def products(chosen, keep):
        packed = call(pack_kernel, shape((3 * PART, WIDE), F32), [vmem] * 3 + [anywhere])(arrived, chosen, keep, panel)
        gathered = lax.all_gather(packed, ("zh", "zl"), axis=0, tiled=True)
        other = lax.ppermute(gathered, "core", [(0, 1), (1, 0)])
        pieces = (BLOCKS, 3 * PART, WIDE)
        cost = (1_000_000_000, 3_000_000)
        full = shape((SLOTS, abs_), F32)
        half = call(mine_kernel, full, [smem] + [vmem] * 2, cost)(place, gathered.reshape(pieces), panel)
        return call(other_kernel, full, [smem] + [vmem] * 3, cost)(place, other.reshape(pieces), panel, half)

    def one_round(number, rank, chosen, keep):
        partial = lax.all_to_all(products(chosen, keep), row, split_axis=0, concat_axis=0, tiled=True)
        copies = call(sum_kernel, shape((4, PART, abs_), F32), [vmem])(partial.reshape(BLOCKS, PART, abs_))
        summed = lax.all_to_all(copies.reshape(CAP, abs_), "y", split_axis=0, concat_axis=0, tiled=True)
        return call(expand_kernel, shape((BLOCK, abs_), F32), [smem] * 2 + [vmem] * 4)(
            place, number, summed, rank, ij, ab
        )

    start = jnp.zeros((1,), I32)
    most, rank, chosen, keep = tables(start)
    out = one_round(start, rank, chosen, keep)

    def again(state):
        number, out = state
        return number + 1, out + one_round(number[None], *tables(number[None])[1:])

    return lax.while_loop(lambda state: state[0] * CAP <= most[0], again, (jnp.int32(1), out))[1]


def solution(mesh):
    finer = Mesh(mesh.devices.reshape(4, 4, 4, 4, 2), ("x", "y", "zh", "zl", "core"))
    col = ("zh", "zl", "core")
    in_specs = (P(col + ("x", "y"), None), P(("x", "y"), col), P(), P(("x", "y")), P(col))
    out_specs = P(("x", "y"), col)
    return jax.shard_map(body, mesh=finer, in_specs=in_specs, out_specs=out_specs, check_vma=False)
```

```python
import jax
import jax.numpy as jnp
from jax import lax
from jax.experimental import pallas as pl
from jax.experimental.pallas import tpu as pltpu
from jax.sharding import Mesh
from jax.sharding import PartitionSpec as P

BLOCK = 128
BLOCKS = 16
LABELS = 8
GROUP = 4
GROUPS = BLOCKS // GROUP
CAP = 160
PART = CAP // 4
SLOTS = GROUPS * CAP
AWAY = (0, 3, -3, 6, -6)
CD_DEV = 96
WIDE = 128
F32, BF16, I32 = jnp.float32, jnp.bfloat16, jnp.int32


def call(kernel, out_shape, in_specs=None, cost=(1_000_000, 1_000_000), **kwargs):
    return pl.pallas_call(
        kernel,
        out_shape=out_shape,
        compiler_params=pltpu.CompilerParams(vmem_limit_bytes=48 * 1024 * 1024),
        cost_estimate=pl.CostEstimate(flops=cost[0], bytes_accessed=cost[1], transcendentals=0),
        **({} if in_specs is None else {"in_specs": in_specs}),
        **kwargs,
    )


def split3(x):
    hi = x.astype(BF16)
    rest = x - hi.astype(F32)
    mid = rest.astype(BF16)
    return hi, mid, (rest - mid.astype(F32)).astype(BF16)


def down(row):
    return jnp.transpose(jnp.broadcast_to(row, (BLOCK, BLOCK)))


def deal_kernel(x_ref, out_ref):
    rows = BLOCKS
    for z in range(GROUP):
        for core in range(2):
            for row in range(rows):
                start = ((row * GROUP + z) * 2 + core) * CD_DEV
                to = (z * 2 + core) * rows + row
                if start + WIDE <= x_ref.shape[1]:
                    out_ref[to] = x_ref[:, start : start + WIDE]
                else:
                    rest = jnp.zeros((x_ref.shape[0], WIDE - CD_DEV), F32)
                    out_ref[to] = jnp.concatenate([x_ref[:, start : start + CD_DEV], rest], axis=1)


def ranks(ij):
    label = lax.broadcasted_iota(I32, (BLOCKS, LABELS, BLOCK), 1)
    same = (jnp.broadcast_to(ij[:, None, :], label.shape) == label).astype(F32)
    upto = lax.broadcasted_iota(I32, (BLOCK, BLOCK), 0) <= lax.broadcasted_iota(I32, (BLOCK, BLOCK), 1)
    count = jnp.dot(
        same.reshape(BLOCKS * LABELS, BLOCK).astype(BF16), upto.astype(BF16), preferred_element_type=F32
    ).reshape(BLOCKS, LABELS, BLOCK)
    rows = []
    for b in range(BLOCKS):
        if b % GROUP == 0:
            before = jnp.zeros((1, LABELS, 1), F32)
        rows.append(jnp.sum((count[b : b + 1] - 1.0 + before) * same[b : b + 1], axis=1))
        before = before + count[b : b + 1, :, BLOCK - 1 :]
    return jnp.concatenate(rows, axis=0)


def table_kernel(place_ref, round_ref, ij_ref, cd_ref, most_ref, rank_ref, chosen_ref, keep_ref):
    core, z, group = place_ref[0], place_ref[1], place_ref[2]
    rank = ranks(ij_ref[...])
    most_ref[0] = jnp.max(rank).astype(I32)
    rank_ref[...] = rank.astype(I32)
    cd = cd_ref[pl.ds(z * 2 + core, 1), :]
    want = lax.broadcasted_iota(I32, (CAP, BLOCK), 0)
    for b in range(GROUP):
        at = slice(b * BLOCK, (b + 1) * BLOCK)
        here = rank_ref[pl.ds(group * GROUP + b, 1), :] - round_ref[0] * CAP
        chosen_ref[:, at] = jnp.where(want == here, 1.0, 0.0).astype(BF16)
        keep_ref[at, :] = jnp.where(down(ij_ref[pl.ds(group * GROUP + b, 1), :]) == cd, 1.0, 0.0)


def pack_kernel(x_ref, chosen_ref, keep_ref, first_ref, out_ref):
    total = jnp.zeros((CAP, WIDE), F32)
    for b in range(GROUP):
        at = slice(b * BLOCK, (b + 1) * BLOCK)
        x = x_ref[b * 32 : (b + 1) * 32].reshape(BLOCK, WIDE)
        x = jnp.where(keep_ref[at, :] > 0.0, x, 0.0)
        hi = x.astype(BF16)
        lo = (x - hi.astype(F32)).astype(BF16)
        for part in (hi, lo):
            total += jnp.dot(chosen_ref[:, at], part, preferred_element_type=F32)
    lane = lax.broadcasted_iota(I32, (PART, WIDE), 1)
    last = total[3 * PART :]
    for k in range(3):
        at = slice(k * PART, (k + 1) * PART)
        out_ref[at, :] = jnp.where(lane < CD_DEV, total[at], pltpu.roll(last, 96 - 32 * k, 1))


def join_kernel(*refs):
    for k, ref in enumerate(refs[:-1]):
        refs[-1][k] = ref[...]


def order_kernel(place_ref, held_ref, above_ref, below_ref, far_ref, out_ref):
    z = place_ref[2] * GROUP + place_ref[1]
    for at, ref in ((z, held_ref), (z + 1, above_ref), (z - 1, below_ref)):
        for k, away in enumerate(AWAY):
            out_ref[(at + away) & (BLOCKS - 1)] = ref[k]
    out_ref[(z + 8) & (BLOCKS - 1)] = far_ref[...]


def from_z(value, step):
    return lax.ppermute(value, ("zh", "zl"), [((z + step) % BLOCKS, z) for z in range(BLOCKS)])


def panel_kernel(v_ref, cd_ref, ab_ref, hi_ref, lo_ref, kept_ref):
    for j in range(v_ref.shape[0] // BLOCK):
        cd = down(cd_ref[j : j + 1, :])
        for k in range(v_ref.shape[1] // BLOCK):
            at = (slice(j * BLOCK, (j + 1) * BLOCK), slice(k * BLOCK, (k + 1) * BLOCK))
            kept_ref[at] = jnp.where(cd == ab_ref[:, at[1]], v_ref[at], 0.0)
    nothing = jnp.zeros((WIDE - CD_DEV, v_ref.shape[1]), BF16)
    for core in range(2):
        for z in range(GROUP):
            start, to = (z * 2 + core) * CD_DEV, (core * GROUP + z) * WIDE
            v = kept_ref[start : start + CD_DEV, :]
            hi = v.astype(BF16)
            hi_ref[to : to + CD_DEV, :] = hi
            lo_ref[to : to + CD_DEV, :] = (v - hi.astype(F32)).astype(BF16)
            hi_ref[to + CD_DEV : to + WIDE, :] = nothing
            lo_ref[to + CD_DEV : to + WIDE, :] = nothing


def unfold(x):
    lane = lax.broadcasted_iota(I32, (PART, WIDE), 1)
    rolled = [pltpu.roll(x[k * PART : (k + 1) * PART], 32 + 32 * k, 1) for k in range(3)]
    last = jnp.where(lane < 32, rolled[0], jnp.where(lane < 64, rolled[1], rolled[2]))
    return jnp.concatenate([x, last], axis=0)


def product(t_ref, core, hi_ref, lo_ref):
    rows = pl.ds(pl.multiple_of(core * GROUP * WIDE, GROUP * WIDE), GROUP * WIDE)
    t = jnp.concatenate(
        [jnp.concatenate([unfold(t_ref[g * GROUP + z]) for z in range(GROUP)], axis=1) for g in range(GROUPS)], axis=0
    )
    t_hi = t.astype(BF16)
    t_lo = (t - t_hi.astype(F32)).astype(BF16)
    total = None
    for a, b in ((t_hi, hi_ref), (t_hi, lo_ref), (t_lo, hi_ref)):
        term = jnp.dot(a, b[rows, :], preferred_element_type=F32)
        total = term if total is None else total + term
    return total


def mine_kernel(place_ref, t_ref, hi_ref, lo_ref, out_ref):
    out_ref[...] = product(t_ref, place_ref[0], hi_ref, lo_ref)


def other_kernel(place_ref, t_ref, hi_ref, lo_ref, mine_ref, out_ref):
    out_ref[...] = mine_ref[...] + product(t_ref, 1 - place_ref[0], hi_ref, lo_ref)


def sum_kernel(x_ref, copies_ref):
    total = x_ref[0]
    for b in range(1, BLOCKS):
        total = total + x_ref[b]
    for b in range(copies_ref.shape[0]):
        copies_ref[b] = total


def spread(a, slots, labels, ab_ref, out_ref):
    chosen = jnp.where(lax.broadcasted_iota(I32, (a.shape[0], BLOCK), 0) == slots, 1.0, 0.0).astype(BF16)
    total = None
    for part in split3(a):
        term = lax.dot_general(chosen, part, (((0,), (0,)), ((), ())), preferred_element_type=F32)
        total = term if total is None else total + term
    ij = down(labels)
    for k in range(out_ref.shape[1] // BLOCK):
        cols = slice(k * BLOCK, (k + 1) * BLOCK)
        out_ref[:, cols] = jnp.where(ij == ab_ref[:, cols], 0.5 * total[:, cols], 0.0)


def expand_kernel(place_ref, round_ref, a_ref, rank_ref, ij_ref, ab_ref, out_ref):
    row = place_ref[3]
    slots = rank_ref[pl.ds(row, 1), :] - round_ref[0] * CAP
    spread(a_ref[...], slots, ij_ref[pl.ds(row, 1), :], ab_ref, out_ref)


def body(amplitudes, integrals, ij_irrep, cd_irrep, ab_irrep):
    smem = pl.BlockSpec(memory_space=pltpu.SMEM)
    vmem = pl.BlockSpec(memory_space=pltpu.VMEM)
    anywhere = pl.BlockSpec(memory_space=pl.ANY)
    shape = jax.ShapeDtypeStruct
    row = ("x", "y")
    place = jnp.stack([lax.axis_index(axis) for axis in ("core", "zl", "zh", row)]).astype(I32)
    ij = ij_irrep.reshape(BLOCKS, BLOCK)
    cd = cd_irrep.reshape(-1, BLOCK)
    cd_own = jnp.pad(cd_irrep.reshape(-1, CD_DEV), ((0, 0), (0, WIDE - CD_DEV)), constant_values=-1)
    ab = ab_irrep.reshape(1, -1)
    cds, abs_ = integrals.shape
    devices = 2 * GROUP * BLOCKS

    dealt = call(deal_kernel, shape((devices, 4, WIDE), F32), [vmem])(amplitudes)
    arrived = lax.all_to_all(dealt, ("zl", "core", "x", "y"), split_axis=0, concat_axis=0, tiled=True)
    v_hi, v_lo = call(
        panel_kernel,
        [shape((2 * GROUP * WIDE, abs_), BF16)] * 2,
        [vmem] * 3,
        (2_000_000, 3_200_000),
        scratch_shapes=[pltpu.VMEM((cds, abs_), F32)],
    )(integrals, cd, ab)

    def tables(number):
        return call(
            table_kernel,
            [
                shape((1,), I32),
                shape((BLOCKS, BLOCK), I32),
                shape((CAP, GROUP * BLOCK), BF16),
                shape((GROUP * BLOCK, WIDE), F32),
            ],
            [smem, smem, vmem, vmem],
            out_specs=[smem, vmem, vmem, vmem],
        )(place, number, ij, cd_own)

    def products(chosen, keep):
        packed = call(pack_kernel, shape((3 * PART, WIDE), F32), [vmem] * 3 + [anywhere])(arrived, chosen, keep, v_hi)
        pieces = (BLOCKS, 3 * PART, WIDE)
        first = [packed] + [from_z(packed, away) for away in AWAY[1:]]
        held = call(join_kernel, shape((len(AWAY),) + pieces[1:], F32), [vmem] * len(AWAY))(*first)
        above, below, far = from_z(held, 1), from_z(held, -1), from_z(first[3], 2)
        gathered = call(order_kernel, shape(pieces, F32), [smem] + [vmem] * 4)(place, held, above, below, far)
        other = lax.ppermute(gathered, "core", [(0, 1), (1, 0)])
        cost = (1_000_000_000, 3_000_000)
        full = shape((SLOTS, abs_), F32)
        half = call(mine_kernel, full, [smem] + [vmem] * 3, cost)(place, gathered, v_hi, v_lo)
        return call(other_kernel, full, [smem] + [vmem] * 4, cost)(place, other, v_hi, v_lo, half)

    def one_round(number, rank, chosen, keep):
        partial = lax.all_to_all(products(chosen, keep), row, split_axis=0, concat_axis=0, tiled=True)
        copies = call(sum_kernel, shape((4, PART, abs_), F32), [vmem])(partial.reshape(BLOCKS, PART, abs_))
        summed = lax.all_to_all(copies.reshape(CAP, abs_), "y", split_axis=0, concat_axis=0, tiled=True)
        return call(expand_kernel, shape((BLOCK, abs_), F32), [smem] * 2 + [vmem] * 4)(
            place, number, summed, rank, ij, ab
        )

    start = jnp.zeros((1,), I32)
    most, rank, chosen, keep = tables(start)
    out = one_round(start, rank, chosen, keep)

    def again(state):
        number, out = state
        return number + 1, out + one_round(number[None], *tables(number[None])[1:])

    return lax.while_loop(lambda state: state[0] * CAP <= most[0], again, (jnp.int32(1), out))[1]


def solution(mesh):
    finer = Mesh(mesh.devices.reshape(4, 4, 4, 4, 2), ("x", "y", "zh", "zl", "core"))
    col = ("zh", "zl", "core")
    in_specs = (P(col + ("x", "y"), None), P(("x", "y"), col), P(), P(("x", "y")), P(col))
    out_specs = P(("x", "y"), col)
    return jax.shard_map(body, mesh=finer, in_specs=in_specs, out_specs=out_specs, check_vma=False)
```

```python
import jax
import jax.numpy as jnp
from jax import lax
from jax.experimental import pallas as pl
from jax.experimental.pallas import tpu as pltpu
from jax.sharding import Mesh
from jax.sharding import PartitionSpec as P

BLOCK = 128
BLOCKS = 16
LABELS = 8
GROUP = 4
GROUPS = BLOCKS // GROUP
CAP = 160
PART = CAP // 4
SLOTS = GROUPS * CAP
CD_DEV = 96
WIDE = 128
F32, BF16, I32 = jnp.float32, jnp.bfloat16, jnp.int32


def call(kernel, out_shape, in_specs=None, cost=(1_000_000, 1_000_000), **kwargs):
    return pl.pallas_call(
        kernel,
        out_shape=out_shape,
        compiler_params=pltpu.CompilerParams(vmem_limit_bytes=48 * 1024 * 1024),
        cost_estimate=pl.CostEstimate(flops=cost[0], bytes_accessed=cost[1], transcendentals=0),
        **({} if in_specs is None else {"in_specs": in_specs}),
        **kwargs,
    )


def split3(x):
    hi = x.astype(BF16)
    rest = x - hi.astype(F32)
    mid = rest.astype(BF16)
    return hi, mid, (rest - mid.astype(F32)).astype(BF16)


def down(row):
    return jnp.transpose(jnp.broadcast_to(row, (BLOCK, BLOCK)))


def deal_kernel(x_ref, out_ref):
    rows = BLOCKS
    for z in range(GROUP):
        for core in range(2):
            for row in range(rows):
                start = ((row * GROUP + z) * 2 + core) * CD_DEV
                to = (z * 2 + core) * rows + row
                if start + WIDE <= x_ref.shape[1]:
                    out_ref[to] = x_ref[:, start : start + WIDE]
                else:
                    rest = jnp.zeros((x_ref.shape[0], WIDE - CD_DEV), F32)
                    out_ref[to] = jnp.concatenate([x_ref[:, start : start + CD_DEV], rest], axis=1)


def ranks(ij):
    label = lax.broadcasted_iota(I32, (BLOCKS, LABELS, BLOCK), 1)
    same = (jnp.broadcast_to(ij[:, None, :], label.shape) == label).astype(F32)
    upto = lax.broadcasted_iota(I32, (BLOCK, BLOCK), 0) <= lax.broadcasted_iota(I32, (BLOCK, BLOCK), 1)
    count = jnp.dot(
        same.reshape(BLOCKS * LABELS, BLOCK).astype(BF16), upto.astype(BF16), preferred_element_type=F32
    ).reshape(BLOCKS, LABELS, BLOCK)
    rows = []
    for b in range(BLOCKS):
        if b % GROUP == 0:
            before = jnp.zeros((1, LABELS, 1), F32)
        rows.append(jnp.sum((count[b : b + 1] - 1.0 + before) * same[b : b + 1], axis=1))
        before = before + count[b : b + 1, :, BLOCK - 1 :]
    return jnp.concatenate(rows, axis=0)


def table_kernel(place_ref, round_ref, ij_ref, cd_ref, ab_ref, most_ref, chosen_ref, keep_ref, spot_ref, like_ref):
    core, z, group, row = place_ref[0], place_ref[1], place_ref[2], place_ref[3]
    rank = ranks(ij_ref[...])
    most_ref[0] = jnp.max(rank).astype(I32)
    rank = rank.astype(I32) - round_ref[0] * CAP
    want = lax.broadcasted_iota(I32, (CAP, BLOCK), 0)
    block = lax.broadcasted_iota(I32, rank.shape, 0)

    def row_of(index):
        return jnp.sum(jnp.where(block == index, rank, 0), axis=0, keepdims=True)

    cd = cd_ref[pl.ds(z * 2 + core, 1), :]
    for b in range(GROUP):
        at = slice(b * BLOCK, (b + 1) * BLOCK)
        chosen_ref[:, at] = jnp.where(want == row_of(group * GROUP + b), 1.0, 0.0).astype(BF16)
        keep_ref[at, :] = jnp.where(down(ij_ref[pl.ds(group * GROUP + b, 1), :]) == cd, 1.0, 0.0)
    spot_ref[...] = jnp.where(want == row_of(row), 1.0, 0.0).astype(BF16)
    ij = down(ij_ref[pl.ds(row, 1), :])
    for k in range(like_ref.shape[1] // BLOCK):
        at = slice(k * BLOCK, (k + 1) * BLOCK)
        like_ref[:, at] = jnp.where(ij == ab_ref[:, at], 1.0, 0.0)


def pack_kernel(x_ref, chosen_ref, keep_ref, first_ref, out_ref):
    total = jnp.zeros((CAP, WIDE), F32)
    for b in range(GROUP):
        at = slice(b * BLOCK, (b + 1) * BLOCK)
        x = x_ref[b * 32 : (b + 1) * 32].reshape(BLOCK, WIDE)
        x = jnp.where(keep_ref[at, :] > 0.0, x, 0.0)
        hi = x.astype(BF16)
        lo = (x - hi.astype(F32)).astype(BF16)
        for part in (hi, lo):
            total += jnp.dot(chosen_ref[:, at], part, preferred_element_type=F32)
    lane = lax.broadcasted_iota(I32, (PART, WIDE), 1)
    last = total[3 * PART :]
    for k in range(3):
        at = slice(k * PART, (k + 1) * PART)
        out_ref[at, :] = jnp.where(lane < CD_DEV, total[at], pltpu.roll(last, 96 - 32 * k, 1))


def panel_kernel(v_ref, cd_ref, ab_ref, hi_ref, lo_ref, kept_ref):
    for j in range(v_ref.shape[0] // BLOCK):
        cd = down(cd_ref[j : j + 1, :])
        for k in range(v_ref.shape[1] // BLOCK):
            at = (slice(j * BLOCK, (j + 1) * BLOCK), slice(k * BLOCK, (k + 1) * BLOCK))
            kept_ref[at] = jnp.where(cd == ab_ref[:, at[1]], v_ref[at], 0.0)
    nothing = jnp.zeros((WIDE - CD_DEV, v_ref.shape[1]), BF16)
    for core in range(2):
        for z in range(GROUP):
            start, to = (z * 2 + core) * CD_DEV, (core * GROUP + z) * WIDE
            v = kept_ref[start : start + CD_DEV, :]
            hi = v.astype(BF16)
            hi_ref[to : to + CD_DEV, :] = hi
            lo_ref[to : to + CD_DEV, :] = (v - hi.astype(F32)).astype(BF16)
            hi_ref[to + CD_DEV : to + WIDE, :] = nothing
            lo_ref[to + CD_DEV : to + WIDE, :] = nothing


def unfold(x):
    lane = lax.broadcasted_iota(I32, (PART, WIDE), 1)
    rolled = [pltpu.roll(x[k * PART : (k + 1) * PART], 32 + 32 * k, 1) for k in range(3)]
    last = jnp.where(lane < 32, rolled[0], jnp.where(lane < 64, rolled[1], rolled[2]))
    return jnp.concatenate([x, last], axis=0)


def product(t_ref, core, hi_ref, lo_ref):
    rows = pl.ds(pl.multiple_of(core * GROUP * WIDE, GROUP * WIDE), GROUP * WIDE)
    t = jnp.concatenate(
        [jnp.concatenate([unfold(t_ref[g * GROUP + z]) for z in range(GROUP)], axis=1) for g in range(GROUPS)], axis=0
    )
    t_hi = t.astype(BF16)
    t_lo = (t - t_hi.astype(F32)).astype(BF16)
    total = None
    for a, b in ((t_hi, hi_ref), (t_hi, lo_ref), (t_lo, hi_ref)):
        term = jnp.dot(a, b[rows, :], preferred_element_type=F32)
        total = term if total is None else total + term
    return total


def mine_kernel(place_ref, t_ref, hi_ref, lo_ref, out_ref):
    out_ref[...] = product(t_ref, place_ref[0], hi_ref, lo_ref)


def other_kernel(place_ref, t_ref, hi_ref, lo_ref, mine_ref, out_ref):
    out_ref[...] = mine_ref[...] + product(t_ref, 1 - place_ref[0], hi_ref, lo_ref)


def sum_kernel(x_ref, copies_ref):
    total = x_ref[0]
    for b in range(1, BLOCKS):
        total = total + x_ref[b]
    for b in range(copies_ref.shape[0]):
        copies_ref[b] = total


def expand_kernel(a_ref, spot_ref, like_ref, out_ref):
    total = None
    for part in split3(a_ref[...]):
        term = lax.dot_general(spot_ref[...], part, (((0,), (0,)), ((), ())), preferred_element_type=F32)
        total = term if total is None else total + term
    out_ref[...] = jnp.where(like_ref[...] > 0.0, 0.5 * total, 0.0)


def body(amplitudes, integrals, ij_irrep, cd_irrep, ab_irrep):
    smem = pl.BlockSpec(memory_space=pltpu.SMEM)
    vmem = pl.BlockSpec(memory_space=pltpu.VMEM)
    anywhere = pl.BlockSpec(memory_space=pl.ANY)
    shape = jax.ShapeDtypeStruct
    row = ("x", "y")
    place = jnp.stack([lax.axis_index(axis) for axis in ("core", "zl", "zh", row)]).astype(I32)
    ij = ij_irrep.reshape(BLOCKS, BLOCK)
    cd = cd_irrep.reshape(-1, BLOCK)
    cd_own = jnp.pad(cd_irrep.reshape(-1, CD_DEV), ((0, 0), (0, WIDE - CD_DEV)), constant_values=-1)
    ab = ab_irrep.reshape(1, -1)
    cds, abs_ = integrals.shape
    devices = 2 * GROUP * BLOCKS

    dealt = call(deal_kernel, shape((devices, 4, WIDE), F32), [vmem])(amplitudes)
    arrived = lax.all_to_all(dealt, ("zl", "core", "x", "y"), split_axis=0, concat_axis=0, tiled=True)
    v_hi, v_lo = call(
        panel_kernel,
        [shape((2 * GROUP * WIDE, abs_), BF16)] * 2,
        [vmem] * 3,
        (2_000_000, 3_200_000),
        scratch_shapes=[pltpu.VMEM((cds, abs_), F32)],
    )(integrals, cd, ab)

    def tables(number):
        return call(
            table_kernel,
            [
                shape((1,), I32),
                shape((CAP, GROUP * BLOCK), BF16),
                shape((GROUP * BLOCK, WIDE), F32),
                shape((CAP, BLOCK), BF16),
                shape((BLOCK, abs_), F32),
            ],
            [smem] * 2 + [vmem] * 3,
            out_specs=[smem] + [vmem] * 4,
        )(place, number, ij, cd_own, ab)

    def products(chosen, keep):
        packed = call(pack_kernel, shape((3 * PART, WIDE), F32), [vmem] * 3 + [anywhere])(arrived, chosen, keep, v_hi)
        gathered = lax.all_gather(packed, ("zh", "zl"), axis=0, tiled=True)
        other = lax.ppermute(gathered, "core", [(0, 1), (1, 0)])
        pieces = (BLOCKS, 3 * PART, WIDE)
        cost = (1_000_000_000, 3_000_000)
        full = shape((SLOTS, abs_), F32)
        half = call(mine_kernel, full, [smem] + [vmem] * 3, cost)(place, gathered.reshape(pieces), v_hi, v_lo)
        return call(other_kernel, full, [smem] + [vmem] * 4, cost)(place, other.reshape(pieces), v_hi, v_lo, half)

    def one_round(chosen, keep, spot, like):
        partial = lax.all_to_all(products(chosen, keep), row, split_axis=0, concat_axis=0, tiled=True)
        copies = call(sum_kernel, shape((4, PART, abs_), F32), [vmem])(partial.reshape(BLOCKS, PART, abs_))
        summed = lax.all_to_all(copies.reshape(CAP, abs_), "y", split_axis=0, concat_axis=0, tiled=True)
        return call(expand_kernel, shape((BLOCK, abs_), F32), [vmem] * 3)(summed, spot, like)

    most, *matrices = tables(jnp.zeros((1,), I32))
    out = one_round(*matrices)

    def again(state):
        number, out = state
        return number + 1, out + one_round(*tables(number[None])[1:])

    return lax.while_loop(lambda state: state[0] * CAP <= most[0], again, (jnp.int32(1), out))[1]


def solution(mesh):
    finer = Mesh(mesh.devices.reshape(4, 4, 4, 4, 2), ("x", "y", "zh", "zl", "core"))
    col = ("zh", "zl", "core")
    in_specs = (P(col + ("x", "y"), None), P(("x", "y"), col), P(), P(("x", "y")), P(col))
    out_specs = P(("x", "y"), col)
    return jax.shard_map(body, mesh=finer, in_specs=in_specs, out_specs=out_specs, check_vma=False)
```

```python
import jax
import jax.numpy as jnp
from jax import lax
from jax.experimental import pallas as pl
from jax.experimental.pallas import tpu as pltpu
from jax.sharding import Mesh
from jax.sharding import PartitionSpec as P

BLOCK = 128
BLOCKS = 16
LABELS = 8
GROUP = 4
GROUPS = BLOCKS // GROUP
CAP = 160
PART = CAP // 4
SLOTS = GROUPS * CAP
CD_DEV = 96
WIDE = 128
F32, BF16, I32 = jnp.float32, jnp.bfloat16, jnp.int32


def call(kernel, out_shape, in_specs=None, cost=(1_000_000, 1_000_000), **kwargs):
    return pl.pallas_call(
        kernel,
        out_shape=out_shape,
        compiler_params=pltpu.CompilerParams(vmem_limit_bytes=48 * 1024 * 1024),
        cost_estimate=pl.CostEstimate(flops=cost[0], bytes_accessed=cost[1], transcendentals=0),
        **({} if in_specs is None else {"in_specs": in_specs}),
        **kwargs,
    )


def split3(x):
    hi = x.astype(BF16)
    rest = x - hi.astype(F32)
    mid = rest.astype(BF16)
    return hi, mid, (rest - mid.astype(F32)).astype(BF16)


def down(row):
    return jnp.transpose(jnp.broadcast_to(row, (BLOCK, BLOCK)))


def deal_kernel(x_ref, out_ref):
    rows = BLOCKS
    for z in range(GROUP):
        for core in range(2):
            for row in range(rows):
                start = ((row * GROUP + z) * 2 + core) * CD_DEV
                to = (z * 2 + core) * rows + row
                if start + WIDE <= x_ref.shape[1]:
                    out_ref[to] = x_ref[:, start : start + WIDE]
                else:
                    rest = jnp.zeros((x_ref.shape[0], WIDE - CD_DEV), F32)
                    out_ref[to] = jnp.concatenate([x_ref[:, start : start + CD_DEV], rest], axis=1)


def ranks(ij):
    label = lax.broadcasted_iota(I32, (BLOCKS, LABELS, BLOCK), 1)
    same = (jnp.broadcast_to(ij[:, None, :], label.shape) == label).astype(F32)
    upto = lax.broadcasted_iota(I32, (BLOCK, BLOCK), 0) <= lax.broadcasted_iota(I32, (BLOCK, BLOCK), 1)
    count = jnp.dot(
        same.reshape(BLOCKS * LABELS, BLOCK).astype(BF16), upto.astype(BF16), preferred_element_type=F32
    ).reshape(BLOCKS, LABELS, BLOCK)
    rows = []
    for b in range(BLOCKS):
        if b % GROUP == 0:
            before = jnp.zeros((1, LABELS, 1), F32)
        rows.append(jnp.sum((count[b : b + 1] - 1.0 + before) * same[b : b + 1], axis=1))
        before = before + count[b : b + 1, :, BLOCK - 1 :]
    return jnp.concatenate(rows, axis=0)


def table_kernel(place_ref, round_ref, ij_ref, cd_ref, ab_ref, most_ref, next_ref, chosen_ref, keep_ref, spot_ref, like_ref):
    core, z, group, row = place_ref[0], place_ref[1], place_ref[2], place_ref[3]
    rank = ranks(ij_ref[...])
    most_ref[0] = jnp.max(rank).astype(I32)
    next_ref[0] = round_ref[0] + 1
    rank = rank.astype(I32) - round_ref[0] * CAP
    want = lax.broadcasted_iota(I32, (CAP, BLOCK), 0)
    block = lax.broadcasted_iota(I32, rank.shape, 0)

    def row_of(index):
        return jnp.sum(jnp.where(block == index, rank, 0), axis=0, keepdims=True)

    cd = cd_ref[pl.ds(z * 2 + core, 1), :]
    for b in range(GROUP):
        at = slice(b * BLOCK, (b + 1) * BLOCK)
        chosen_ref[:, at] = jnp.where(want == row_of(group * GROUP + b), 1.0, 0.0).astype(BF16)
        keep_ref[at, :] = jnp.where(down(ij_ref[pl.ds(group * GROUP + b, 1), :]) == cd, 1.0, 0.0)
    spot_ref[...] = jnp.where(want == row_of(row), 1.0, 0.0).astype(BF16)
    ij = down(ij_ref[pl.ds(row, 1), :])
    for k in range(like_ref.shape[1] // BLOCK):
        at = slice(k * BLOCK, (k + 1) * BLOCK)
        like_ref[:, at] = jnp.where(ij == ab_ref[:, at], 1.0, 0.0)


def pack_kernel(x_ref, chosen_ref, keep_ref, first_ref, out_ref):
    total = jnp.zeros((CAP, WIDE), F32)
    for b in range(GROUP):
        at = slice(b * BLOCK, (b + 1) * BLOCK)
        x = x_ref[b * 32 : (b + 1) * 32].reshape(BLOCK, WIDE)
        x = jnp.where(keep_ref[at, :] > 0.0, x, 0.0)
        hi = x.astype(BF16)
        lo = (x - hi.astype(F32)).astype(BF16)
        for part in (hi, lo):
            total += jnp.dot(chosen_ref[:, at], part, preferred_element_type=F32)
    lane = lax.broadcasted_iota(I32, (PART, WIDE), 1)
    last = total[3 * PART :]
    for k in range(3):
        at = slice(k * PART, (k + 1) * PART)
        out_ref[at, :] = jnp.where(lane < CD_DEV, total[at], pltpu.roll(last, 96 - 32 * k, 1))


def panel_kernel(v_ref, cd_ref, ab_ref, hi_ref, lo_ref, kept_ref):
    for j in range(v_ref.shape[0] // BLOCK):
        cd = down(cd_ref[j : j + 1, :])
        for k in range(v_ref.shape[1] // BLOCK):
            at = (slice(j * BLOCK, (j + 1) * BLOCK), slice(k * BLOCK, (k + 1) * BLOCK))
            kept_ref[at] = jnp.where(cd == ab_ref[:, at[1]], v_ref[at], 0.0)
    nothing = jnp.zeros((WIDE - CD_DEV, v_ref.shape[1]), BF16)
    for core in range(2):
        for z in range(GROUP):
            start, to = (z * 2 + core) * CD_DEV, (core * GROUP + z) * WIDE
            v = kept_ref[start : start + CD_DEV, :]
            hi = v.astype(BF16)
            hi_ref[to : to + CD_DEV, :] = hi
            lo_ref[to : to + CD_DEV, :] = (v - hi.astype(F32)).astype(BF16)
            hi_ref[to + CD_DEV : to + WIDE, :] = nothing
            lo_ref[to + CD_DEV : to + WIDE, :] = nothing


def unfold(x):
    lane = lax.broadcasted_iota(I32, (PART, WIDE), 1)
    rolled = [pltpu.roll(x[k * PART : (k + 1) * PART], 32 + 32 * k, 1) for k in range(3)]
    last = jnp.where(lane < 32, rolled[0], jnp.where(lane < 64, rolled[1], rolled[2]))
    return jnp.concatenate([x, last], axis=0)


def product(t_ref, core, hi_ref, lo_ref):
    rows = pl.ds(pl.multiple_of(core * GROUP * WIDE, GROUP * WIDE), GROUP * WIDE)
    t = jnp.concatenate(
        [jnp.concatenate([unfold(t_ref[g * GROUP + z]) for z in range(GROUP)], axis=1) for g in range(GROUPS)], axis=0
    )
    t_hi = t.astype(BF16)
    t_lo = (t - t_hi.astype(F32)).astype(BF16)
    total = None
    for a, b in ((t_hi, hi_ref), (t_hi, lo_ref), (t_lo, hi_ref)):
        term = jnp.dot(a, b[rows, :], preferred_element_type=F32)
        total = term if total is None else total + term
    return total


def mine_kernel(place_ref, t_ref, hi_ref, lo_ref, out_ref):
    out_ref[...] = product(t_ref, place_ref[0], hi_ref, lo_ref)


def other_kernel(place_ref, t_ref, hi_ref, lo_ref, mine_ref, out_ref):
    out_ref[...] = mine_ref[...] + product(t_ref, 1 - place_ref[0], hi_ref, lo_ref)


def sum_kernel(x_ref, copies_ref):
    total = x_ref[0]
    for b in range(1, BLOCKS):
        total = total + x_ref[b]
    for b in range(copies_ref.shape[0]):
        copies_ref[b] = total


def expand_kernel(a_ref, spot_ref, like_ref, out_ref):
    total = None
    for part in split3(a_ref[...]):
        term = lax.dot_general(spot_ref[...], part, (((0,), (0,)), ((), ())), preferred_element_type=F32)
        total = term if total is None else total + term
    out_ref[...] = jnp.where(like_ref[...] > 0.0, 0.5 * total, 0.0)


def body(amplitudes, integrals, ij_irrep, cd_irrep, ab_irrep):
    smem = pl.BlockSpec(memory_space=pltpu.SMEM)
    vmem = pl.BlockSpec(memory_space=pltpu.VMEM)
    anywhere = pl.BlockSpec(memory_space=pl.ANY)
    shape = jax.ShapeDtypeStruct
    row = ("x", "y")
    place = jnp.stack([lax.axis_index(axis) for axis in ("core", "zl", "zh", row)]).astype(I32)
    ij = ij_irrep.reshape(BLOCKS, BLOCK)
    cd = cd_irrep.reshape(-1, BLOCK)
    cd_own = jnp.pad(cd_irrep.reshape(-1, CD_DEV), ((0, 0), (0, WIDE - CD_DEV)), constant_values=-1)
    ab = ab_irrep.reshape(1, -1)
    cds, abs_ = integrals.shape
    devices = 2 * GROUP * BLOCKS

    dealt = call(deal_kernel, shape((devices, 4, WIDE), F32), [vmem])(amplitudes)
    arrived = lax.all_to_all(dealt, ("zl", "core", "x", "y"), split_axis=0, concat_axis=0, tiled=True)
    v_hi, v_lo = call(
        panel_kernel,
        [shape((2 * GROUP * WIDE, abs_), BF16)] * 2,
        [vmem] * 3,
        (2_000_000, 3_200_000),
        scratch_shapes=[pltpu.VMEM((cds, abs_), F32)],
    )(integrals, cd, ab)

    def tables(number):
        return call(
            table_kernel,
            [
                shape((1,), I32),
                shape((1,), I32),
                shape((CAP, GROUP * BLOCK), BF16),
                shape((GROUP * BLOCK, WIDE), F32),
                shape((CAP, BLOCK), BF16),
                shape((BLOCK, abs_), F32),
            ],
            [smem] * 2 + [vmem] * 3,
            out_specs=[smem] * 2 + [vmem] * 4,
        )(place, number, ij, cd_own, ab)

    def products(chosen, keep):
        packed = call(pack_kernel, shape((3 * PART, WIDE), F32), [vmem] * 3 + [anywhere])(arrived, chosen, keep, v_hi)
        gathered = lax.all_gather(packed, ("zh", "zl"), axis=0, tiled=True)
        other = lax.ppermute(gathered, "core", [(0, 1), (1, 0)])
        pieces = (BLOCKS, 3 * PART, WIDE)
        cost = (1_000_000_000, 3_000_000)
        full = shape((SLOTS, abs_), F32)
        half = call(mine_kernel, full, [smem] + [vmem] * 3, cost)(place, gathered.reshape(pieces), v_hi, v_lo)
        return call(other_kernel, full, [smem] + [vmem] * 4, cost)(place, other.reshape(pieces), v_hi, v_lo, half)

    def one_round(chosen, keep, spot, like):
        partial = lax.all_to_all(products(chosen, keep), row, split_axis=0, concat_axis=0, tiled=True)
        copies = call(sum_kernel, shape((4, PART, abs_), F32), [vmem])(partial.reshape(BLOCKS, PART, abs_))
        summed = lax.all_to_all(copies.reshape(CAP, abs_), "y", split_axis=0, concat_axis=0, tiled=True)
        return call(expand_kernel, shape((BLOCK, abs_), F32), [vmem] * 3)(summed, spot, like)

    most, following, *matrices = tables(jnp.zeros((1,), I32))
    out = one_round(*matrices)

    def again(state):
        number, out = state
        _, following, *matrices = tables(number)
        return following, out + one_round(*matrices)

    return lax.while_loop(lambda state: state[0][0] * CAP <= most[0], again, (following, out))[1]


def solution(mesh):
    finer = Mesh(mesh.devices.reshape(4, 4, 4, 4, 2), ("x", "y", "zh", "zl", "core"))
    col = ("zh", "zl", "core")
    in_specs = (P(col + ("x", "y"), None), P(("x", "y"), col), P(), P(("x", "y")), P(col))
    out_specs = P(("x", "y"), col)
    return jax.shard_map(body, mesh=finer, in_specs=in_specs, out_specs=out_specs, check_vma=False)
```

```python
import jax
import jax.numpy as jnp
from jax import lax
from jax.experimental import pallas as pl
from jax.experimental.pallas import tpu as pltpu
from jax.sharding import Mesh
from jax.sharding import PartitionSpec as P

BLOCK = 128
BLOCKS = 16
LABELS = 8
GROUP = 4
GROUPS = BLOCKS // GROUP
CAP = 160
PART = CAP // 4
SLOTS = GROUPS * CAP
CD_DEV = 96
WIDE = 128
F32, BF16, I32 = jnp.float32, jnp.bfloat16, jnp.int32


def call(kernel, out_shape, in_specs=None, cost=(1_000_000, 1_000_000), **kwargs):
    return pl.pallas_call(
        kernel,
        out_shape=out_shape,
        compiler_params=pltpu.CompilerParams(vmem_limit_bytes=48 * 1024 * 1024),
        cost_estimate=pl.CostEstimate(flops=cost[0], bytes_accessed=cost[1], transcendentals=0),
        **({} if in_specs is None else {"in_specs": in_specs}),
        **kwargs,
    )


def split3(x):
    hi = x.astype(BF16)
    rest = x - hi.astype(F32)
    mid = rest.astype(BF16)
    return hi, mid, (rest - mid.astype(F32)).astype(BF16)


def down(row):
    return jnp.transpose(jnp.broadcast_to(row, (BLOCK, BLOCK)))


def deal_kernel(x_ref, out_ref):
    rows = BLOCKS
    for z in range(GROUP):
        for core in range(2):
            for row in range(rows):
                start = ((row * GROUP + z) * 2 + core) * CD_DEV
                to = (row * GROUP + z) * 2 + core
                if start + WIDE <= x_ref.shape[1]:
                    out_ref[to] = x_ref[:, start : start + WIDE]
                else:
                    rest = jnp.zeros((x_ref.shape[0], WIDE - CD_DEV), F32)
                    out_ref[to] = jnp.concatenate([x_ref[:, start : start + CD_DEV], rest], axis=1)


def ranks(ij):
    label = lax.broadcasted_iota(I32, (BLOCKS, LABELS, BLOCK), 1)
    same = (jnp.broadcast_to(ij[:, None, :], label.shape) == label).astype(F32)
    upto = lax.broadcasted_iota(I32, (BLOCK, BLOCK), 0) <= lax.broadcasted_iota(I32, (BLOCK, BLOCK), 1)
    count = jnp.dot(
        same.reshape(BLOCKS * LABELS, BLOCK).astype(BF16), upto.astype(BF16), preferred_element_type=F32
    ).reshape(BLOCKS, LABELS, BLOCK)
    rows = []
    for b in range(BLOCKS):
        if b % GROUP == 0:
            before = jnp.zeros((1, LABELS, 1), F32)
        rows.append(jnp.sum((count[b : b + 1] - 1.0 + before) * same[b : b + 1], axis=1))
        before = before + count[b : b + 1, :, BLOCK - 1 :]
    return jnp.concatenate(rows, axis=0)


def table_kernel(place_ref, round_ref, ij_ref, cd_ref, ab_ref, most_ref, next_ref, chosen_ref, keep_ref, spot_ref, like_ref):
    core, z, group, row = place_ref[0], place_ref[1], place_ref[2], place_ref[3]
    rank = ranks(ij_ref[...])
    most_ref[0] = jnp.max(rank).astype(I32)
    next_ref[0] = round_ref[0] + 1
    rank = rank.astype(I32) - round_ref[0] * CAP
    want = lax.broadcasted_iota(I32, (CAP, BLOCK), 0)
    block = lax.broadcasted_iota(I32, rank.shape, 0)

    def row_of(index):
        return jnp.sum(jnp.where(block == index, rank, 0), axis=0, keepdims=True)

    cd = cd_ref[pl.ds(z * 2 + core, 1), :]
    for b in range(GROUP):
        at = slice(b * BLOCK, (b + 1) * BLOCK)
        chosen_ref[:, at] = jnp.where(want == row_of(group * GROUP + b), 1.0, 0.0).astype(BF16)
        keep_ref[at, :] = jnp.where(down(ij_ref[pl.ds(group * GROUP + b, 1), :]) == cd, 1.0, 0.0)
    spot_ref[...] = jnp.where(want == row_of(row), 1.0, 0.0).astype(BF16)
    ij = down(ij_ref[pl.ds(row, 1), :])
    for k in range(like_ref.shape[1] // BLOCK):
        at = slice(k * BLOCK, (k + 1) * BLOCK)
        like_ref[:, at] = jnp.where(ij == ab_ref[:, at], 1.0, 0.0)


def pack_kernel(x_ref, chosen_ref, keep_ref, first_ref, out_ref):
    total = jnp.zeros((CAP, WIDE), F32)
    for b in range(GROUP):
        at = slice(b * BLOCK, (b + 1) * BLOCK)
        x = jnp.concatenate([x_ref[:, 2 * b + core].reshape(BLOCK // 2, WIDE) for core in range(2)], axis=0)
        x = jnp.where(keep_ref[at, :] > 0.0, x, 0.0)
        hi = x.astype(BF16)
        lo = (x - hi.astype(F32)).astype(BF16)
        for part in (hi, lo):
            total += jnp.dot(chosen_ref[:, at], part, preferred_element_type=F32)
    lane = lax.broadcasted_iota(I32, (PART, WIDE), 1)
    last = total[3 * PART :]
    for k in range(3):
        at = slice(k * PART, (k + 1) * PART)
        out_ref[at, :] = jnp.where(lane < CD_DEV, total[at], pltpu.roll(last, 96 - 32 * k, 1))


def panel_kernel(v_ref, cd_ref, ab_ref, hi_ref, lo_ref, kept_ref):
    for j in range(v_ref.shape[0] // BLOCK):
        cd = down(cd_ref[j : j + 1, :])
        for k in range(v_ref.shape[1] // BLOCK):
            at = (slice(j * BLOCK, (j + 1) * BLOCK), slice(k * BLOCK, (k + 1) * BLOCK))
            kept_ref[at] = jnp.where(cd == ab_ref[:, at[1]], v_ref[at], 0.0)
    nothing = jnp.zeros((WIDE - CD_DEV, v_ref.shape[1]), BF16)
    for core in range(2):
        for z in range(GROUP):
            start, to = (z * 2 + core) * CD_DEV, (core * GROUP + z) * WIDE
            v = kept_ref[start : start + CD_DEV, :]
            hi = v.astype(BF16)
            hi_ref[to : to + CD_DEV, :] = hi
            lo_ref[to : to + CD_DEV, :] = (v - hi.astype(F32)).astype(BF16)
            hi_ref[to + CD_DEV : to + WIDE, :] = nothing
            lo_ref[to + CD_DEV : to + WIDE, :] = nothing


def unfold(x):
    lane = lax.broadcasted_iota(I32, (PART, WIDE), 1)
    rolled = [pltpu.roll(x[k * PART : (k + 1) * PART], 32 + 32 * k, 1) for k in range(3)]
    last = jnp.where(lane < 32, rolled[0], jnp.where(lane < 64, rolled[1], rolled[2]))
    return jnp.concatenate([x, last], axis=0)


def product(t_ref, core, hi_ref, lo_ref):
    rows = pl.ds(pl.multiple_of(core * GROUP * WIDE, GROUP * WIDE), GROUP * WIDE)
    t = jnp.concatenate(
        [jnp.concatenate([unfold(t_ref[g * GROUP + z]) for z in range(GROUP)], axis=1) for g in range(GROUPS)], axis=0
    )
    t_hi = t.astype(BF16)
    t_lo = (t - t_hi.astype(F32)).astype(BF16)
    total = None
    for a, b in ((t_hi, hi_ref), (t_hi, lo_ref), (t_lo, hi_ref)):
        term = jnp.dot(a, b[rows, :], preferred_element_type=F32)
        total = term if total is None else total + term
    return total


def mine_kernel(place_ref, t_ref, hi_ref, lo_ref, out_ref):
    out_ref[...] = product(t_ref, place_ref[0], hi_ref, lo_ref)


def other_kernel(place_ref, t_ref, hi_ref, lo_ref, mine_ref, out_ref):
    out_ref[...] = mine_ref[...] + product(t_ref, 1 - place_ref[0], hi_ref, lo_ref)


def sum_kernel(x_ref, copies_ref):
    total = x_ref[0]
    for b in range(1, BLOCKS):
        total = total + x_ref[b]
    for b in range(copies_ref.shape[0]):
        copies_ref[b] = total


def expand_kernel(a_ref, spot_ref, like_ref, out_ref):
    total = None
    for part in split3(a_ref[...]):
        term = lax.dot_general(spot_ref[...], part, (((0,), (0,)), ((), ())), preferred_element_type=F32)
        total = term if total is None else total + term
    out_ref[...] = jnp.where(like_ref[...] > 0.0, 0.5 * total, 0.0)


def body(amplitudes, integrals, ij_irrep, cd_irrep, ab_irrep):
    smem = pl.BlockSpec(memory_space=pltpu.SMEM)
    vmem = pl.BlockSpec(memory_space=pltpu.VMEM)
    anywhere = pl.BlockSpec(memory_space=pl.ANY)
    shape = jax.ShapeDtypeStruct
    row = ("x", "y")
    place = jnp.stack([lax.axis_index(axis) for axis in ("core", "zl", "zh", row)]).astype(I32)
    ij = ij_irrep.reshape(BLOCKS, BLOCK)
    cd = cd_irrep.reshape(-1, BLOCK)
    cd_own = jnp.pad(cd_irrep.reshape(-1, CD_DEV), ((0, 0), (0, WIDE - CD_DEV)), constant_values=-1)
    ab = ab_irrep.reshape(1, -1)
    cds, abs_ = integrals.shape
    devices = 2 * GROUP * BLOCKS

    dealt = call(deal_kernel, shape((devices, 4, WIDE), F32), [vmem])(amplitudes)
    arrived = lax.all_to_all(dealt, ("x", "y", "zl", "core"), split_axis=0, concat_axis=0, tiled=True)
    arrived = arrived.reshape(BLOCKS, 2 * GROUP, 4, WIDE)
    v_hi, v_lo = call(
        panel_kernel,
        [shape((2 * GROUP * WIDE, abs_), BF16)] * 2,
        [vmem] * 3,
        (2_000_000, 3_200_000),
        scratch_shapes=[pltpu.VMEM((cds, abs_), F32)],
    )(integrals, cd, ab)

    def tables(number):
        return call(
            table_kernel,
            [
                shape((1,), I32),
                shape((1,), I32),
                shape((CAP, GROUP * BLOCK), BF16),
                shape((GROUP * BLOCK, WIDE), F32),
                shape((CAP, BLOCK), BF16),
                shape((BLOCK, abs_), F32),
            ],
            [smem] * 2 + [vmem] * 3,
            out_specs=[smem] * 2 + [vmem] * 4,
        )(place, number, ij, cd_own, ab)

    def products(chosen, keep):
        packed = call(pack_kernel, shape((3 * PART, WIDE), F32), [vmem] * 3 + [anywhere])(arrived, chosen, keep, v_hi)
        gathered = lax.all_gather(packed, ("zh", "zl"), axis=0, tiled=True)
        other = lax.ppermute(gathered, "core", [(0, 1), (1, 0)])
        pieces = (BLOCKS, 3 * PART, WIDE)
        cost = (1_000_000_000, 3_000_000)
        full = shape((SLOTS, abs_), F32)
        half = call(mine_kernel, full, [smem] + [vmem] * 3, cost)(place, gathered.reshape(pieces), v_hi, v_lo)
        return call(other_kernel, full, [smem] + [vmem] * 4, cost)(place, other.reshape(pieces), v_hi, v_lo, half)

    def one_round(chosen, keep, spot, like):
        partial = lax.all_to_all(products(chosen, keep), row, split_axis=0, concat_axis=0, tiled=True)
        copies = call(sum_kernel, shape((4, PART, abs_), F32), [vmem])(partial.reshape(BLOCKS, PART, abs_))
        summed = lax.all_to_all(copies.reshape(CAP, abs_), "y", split_axis=0, concat_axis=0, tiled=True)
        return call(expand_kernel, shape((BLOCK, abs_), F32), [vmem] * 3)(summed, spot, like)

    most, following, *matrices = tables(jnp.zeros((1,), I32))
    out = one_round(*matrices)

    def again(state):
        number, out = state
        _, following, *matrices = tables(number)
        return following, out + one_round(*matrices)

    return lax.while_loop(lambda state: state[0][0] * CAP <= most[0], again, (following, out))[1]


def solution(mesh):
    finer = Mesh(mesh.devices.reshape(4, 4, 4, 4, 2), ("x", "y", "zh", "zl", "core"))
    col = ("zh", "zl", "core")
    in_specs = (P(col + ("x", "y"), None), P(("x", "y"), col), P(), P(("x", "y")), P(col))
    out_specs = P(("x", "y"), col)
    return jax.shard_map(body, mesh=finer, in_specs=in_specs, out_specs=out_specs, check_vma=False)
```
